512 devices in a mesh: batch: 16 (over y_hi, x, core), ctx: 32 (over y_lo, z).
Axes of the slice: x: 4, y: 8 (y_hi: 2, y_lo: 4; y = y_hi * 4 + y_lo), z: 8, core: 2. Of those that a mesh axis runs over, the one named last changes fastest.
Arguments:
- hist_query: bfloat16 [131072, 512], P(('batch', 'ctx')), may hold values from -6 to 6
- hist_key: bfloat16 [131072, 512], P(('batch', 'ctx')), may hold values from -6 to 6
- hist_value: bfloat16 [131072, 512], P(('batch', 'ctx')), may hold values from -6 to 6
- hist_gate: bfloat16 [131072, 512], P(('batch', 'ctx')), may hold values from -6 to 6
- hist_input: bfloat16 [131072, 1024], P(('batch', 'ctx')), may hold values from -6 to 6
- cand_query: bfloat16 [16384, 512], P(('batch', 'ctx')), may hold values from -6 to 6
- cand_key: bfloat16 [16384, 512], P(('batch', 'ctx')), may hold values from -6 to 6
- cand_value: bfloat16 [16384, 512], P(('batch', 'ctx')), may hold values from -6 to 6
- cand_gate: bfloat16 [16384, 512], P(('batch', 'ctx')), may hold values from -6 to 6
- cand_input: bfloat16 [16384, 1024], P(('batch', 'ctx')), may hold values from -6 to 6
- cand_user: int32 [16384], P('batch'), may hold values from 0 to 1
- hist_len: int32 [32], P('batch'), may hold values from 1 to 8064, as said below
- hist_start: int32 [32], P('batch'), may hold values from 0 to 8064, as said below
- out_weight: bfloat16 [512, 1024], replicated, may hold values from -0.25 to 0.25
Outputs:
- hist_out: bfloat16 [131072, 1024], P(('batch', 'ctx'))
- cand_out: bfloat16 [16384, 1024], P(('batch', 'ctx'))
The draws below stay inside these ranges and needn't reach their ends.
Inputs may be any that keep to these rules, and one draw needn't show every extreme that they name: `hist_len`: in each group the users take whole consecutive blocks of 128 slots: the first user starts at slot 0, the next at the block after the first user's last block; a user with b blocks has a length above (b - 1) * 128; slots after the last user's history are padding, and some groups use every block. `hist_start`: multiples of 128; the first user of every group starts at 0. `cand_user`: index of a user of the candidate's own group.
All inputs are finite; a program needn't handle non-finite values.
Results may differ from the reference program's by a relative error of at most 0.006.
Values may be sent and summed in bfloat16 or wider, within the bound.
No kernel may reach another device: no remote copies, remote signals or barrier semaphores. Data moves between devices by JAX's collectives and lax.ppermute only.
A program may use at most 128 MiB of HBM per device.

```python
import math
import jax
import jax.numpy as jnp
from jax import lax

D = 1024
HEADS = 4
DH = 128
BLOCK = 128
BLK_DEV = 2
USERS_GRP = 2
HD = 512
EVENTS = 131072
CANDS = 16384
N_BATCH = 16
N_CTX = 32


def layout(key):
    keys = jax.random.split(key, 3)
    block_count = BLK_DEV * N_CTX
    lowest = max(2, block_count // 4)
    used = jax.random.randint(keys[0], (N_BATCH,), lowest, block_count + 1)
    used = used.at[0].set(block_count)
    first = jax.random.randint(keys[1], (N_BATCH,), 1, used)
    first = first.at[0].set(block_count - 1)
    blocks = jnp.stack([first, used - first], axis=1)
    tails = jax.random.randint(keys[2], (N_BATCH, 2), 1, BLOCK + 1)
    tails = tails.at[0, 0].set(BLOCK).at[0, 1].set(1)
    lens = (blocks - 1) * BLOCK + tails
    starts = jnp.stack([jnp.zeros_like(first), first * BLOCK], axis=1)
    return (lens.reshape(-1).astype(jnp.int32), starts.reshape(-1).astype(jnp.int32))


def draw_hist_len(key, part):
    lens, starts = layout(key)
    return lens


def draw_hist_start(key, part):
    lens, starts = layout(key)
    return starts


def touch_ends(drawn, own_key, low, top_value):
    longest = drawn.shape.index(max(drawn.shape))
    spots = []
    for shift in (0, 1):
        where = [jax.random.randint(jax.random.fold_in(own_key, axis), (), 0, length) for axis, length in enumerate(drawn.shape)]
        where[longest] = (where[longest] + shift) % drawn.shape[longest]
        spots.append(tuple(where))
    return drawn.at[spots[0]].set(low).at[spots[1]].set(top_value)


def block_levels(rng, extent, cuts, least, top_value):
    gain = 1.0
    for dim, blocks in cuts:
        steps = jax.random.uniform(jax.random.fold_in(jax.random.fold_in(rng, 6), dim), (blocks,), jnp.float32, least / len(cuts), top_value / len(cuts))
        gain = gain * jnp.repeat(jnp.exp(steps), extent[dim] // blocks).reshape((-1,) + (1,) * (len(extent) - 1 - dim))
    return gain


def normal_values(own_key, shape, deviation, most, pieces=(), kind=jnp.bfloat16):
    values = deviation * jax.random.normal(own_key, shape, jnp.float32)
    if pieces:
        values = values * block_levels(own_key, shape, pieces, -0.22, 0.18)
    return jnp.clip(values, -most, most).astype(kind)


def setup_inputs(seed: int = 0) -> dict:
    key_of = jax.random.split(jax.random.key(seed), 15)
    return {
        "hist_query": normal_values(key_of[0], (EVENTS, HD), 1.0, 6.0, ((0, 512),)),
        "hist_key": normal_values(key_of[1], (EVENTS, HD), 1.0, 6.0, ((0, 512),)),
        "hist_value": normal_values(key_of[2], (EVENTS, HD), 1.0, 6.0, ((0, 512),)),
        "hist_gate": normal_values(key_of[3], (EVENTS, HD), 1.0, 6.0, ((0, 512),)),
        "hist_input": normal_values(key_of[4], (EVENTS, D), 1.0, 6.0, ((0, 512),)),
        "cand_query": normal_values(key_of[5], (CANDS, HD), 1.0, 6.0, ((0, 512),)),
        "cand_key": normal_values(key_of[6], (CANDS, HD), 1.0, 6.0, ((0, 512),)),
        "cand_value": normal_values(key_of[7], (CANDS, HD), 1.0, 6.0, ((0, 512),)),
        "cand_gate": normal_values(key_of[8], (CANDS, HD), 1.0, 6.0, ((0, 512),)),
        "cand_input": normal_values(key_of[9], (CANDS, D), 1.0, 6.0, ((0, 512),)),
        "cand_user": touch_ends(jax.random.randint(key_of[10], (CANDS,), 0, USERS_GRP), jax.random.fold_in(key_of[10], 1), 0, USERS_GRP - 1).astype(jnp.int32),
        "hist_len": draw_hist_len(jax.random.fold_in(key_of[14], 71), 0),
        "hist_start": draw_hist_start(jax.random.fold_in(key_of[14], 71), 0),
        "out_weight": normal_values(key_of[13], (HD, D), HD ** -0.5, 0.25),
    }


def owners(events, lens, starts):
    result = jnp.full(events.shape, -1, jnp.int32)
    for user in range(lens.shape[0]):
        inside = (events >= starts[user]) & (events < starts[user] + lens[user])
        result = jnp.where(inside, jnp.int32(user), result)
    return result

def pointwise(queries, keys, values, mask):
    rows = queries.shape[0]
    width = queries.shape[1]
    q_heads = queries.reshape(rows, HEADS, DH).astype(jnp.float32)
    k_heads = keys.reshape(keys.shape[0], HEADS, DH).astype(jnp.float32)
    v_heads = values.reshape(values.shape[0], HEADS, DH).astype(jnp.float32)
    scores = jnp.einsum('qhd,khd->hqk', q_heads, k_heads) * (1.0 / math.sqrt(DH))
    weights = jnp.where(mask[None], jax.nn.silu(scores), 0.0).astype(jnp.bfloat16)
    out = jnp.einsum('hqk,khd->qhd', weights.astype(jnp.float32), v_heads)
    return out.reshape(rows, width)

def self_term(queries, keys, values):
    rows = queries.shape[0]
    q_heads = queries.reshape(rows, HEADS, DH).astype(jnp.float32)
    k_heads = keys.reshape(rows, HEADS, DH).astype(jnp.float32)
    v_heads = values.reshape(rows, HEADS, DH).astype(jnp.float32)
    scores = lax.optimization_barrier(jnp.sum(q_heads * k_heads, axis=-1)) * (1.0 / math.sqrt(DH))
    weights = jax.nn.silu(scores).astype(jnp.bfloat16).astype(jnp.float32)
    return (weights[:, :, None] * v_heads).reshape(rows, HEADS * DH)

def finish(total, gate, inputs, out_weight):
    mean = lax.optimization_barrier(jnp.mean(total, axis=-1, keepdims=True))
    centered = total - mean
    spread = lax.optimization_barrier(jnp.mean(centered * centered, axis=-1, keepdims=True))
    normed = centered * lax.rsqrt(spread + 1e-05)
    gated = (normed * gate.astype(jnp.float32)).astype(jnp.bfloat16)
    mixed = jnp.dot(gated, out_weight, preferred_element_type=jnp.float32)
    return (inputs.astype(jnp.float32) + mixed).astype(jnp.bfloat16)

def reference(hist_query, hist_key, hist_value, hist_gate, hist_input, cand_query, cand_key, cand_value, cand_gate, cand_input, cand_user, hist_len, hist_start, out_weight):
    length = BLOCK * BLK_DEV * N_CTX
    block_count = BLK_DEV * N_CTX

    def one_group(group):
        hq, hk, hv, hg, hx, cq, ck, cv, cg, cx, users, lens, starts = group
        events = jnp.arange(length, dtype=jnp.int32)
        owner = owners(events, lens, starts)

        def one_block(index):
            first = (index * BLOCK).astype(jnp.int32)
            rows = lax.dynamic_slice_in_dim(hq, first, BLOCK)
            row_events = first + jnp.arange(BLOCK, dtype=jnp.int32)
            row_owner = lax.dynamic_slice_in_dim(owner, first, BLOCK)
            mask = (row_owner[:, None] == owner[None, :]) & (row_owner[:, None] >= 0) & (events[None, :] <= row_events[:, None])
            return pointwise(rows, hk, hv, mask)
        hist_total = lax.map(one_block, jnp.arange(block_count, dtype=jnp.int32)).reshape(length, HEADS * DH)
        cand_mask = users[:, None] == owner[None, :]
        cand_total = pointwise(cq, hk, hv, cand_mask) + self_term(cq, ck, cv)
        return (finish(hist_total, hg, hx, out_weight), finish(cand_total, cg, cx, out_weight))

    def split(array):
        return array.reshape((N_BATCH, array.shape[0] // N_BATCH) + array.shape[1:])
    group_args = tuple((split(a) for a in (hist_query, hist_key, hist_value, hist_gate, hist_input, cand_query, cand_key, cand_value, cand_gate, cand_input, cand_user, hist_len, hist_start)))
    hist_out, cand_out = lax.map(one_group, group_args)
    return (hist_out.reshape(N_BATCH * length, D), cand_out.reshape(-1, D))
```

```python
import functools
import math

import jax
import jax.numpy as jnp
from jax import lax
from jax.experimental import pallas as pl
from jax.experimental.pallas import tpu as pltpu
from jax.sharding import Mesh, PartitionSpec as P

HEADS = 4
DH = 128
NY = 4
NZ = 8
ROWS = 256
CROWS = 32
QROWS = ROWS + CROWS
STRIP = NZ * ROWS
HALF = 1.0 / (2.0 * math.sqrt(DH))
VMEM_LIMIT = 48 * 1024 * 1024


def contract_lanes(a, b):
    return lax.dot_general(a, b, (((1,), (1,)), ((), ())), preferred_element_type=jnp.float32)


def silu_weight(scores):
    half = scores * HALF
    return half * jnp.tanh(half) + half


def attend_kernel(heads, place_ref, start_ref, len_ref, q0, q1, q2, q3, kv_ref, cu_ref, own_ref, o1, o2, o3, acc, cq, cacc):
    width = heads * DH
    y = place_ref[0]
    z = place_ref[1]
    starts = [start_ref[u] for u in range(2)]
    ends = [start_ref[u] + len_ref[u] for u in range(2)]
    strip0 = y * STRIP
    qs = (q0, q1, q2, q3)

    def cols(h):
        return slice(h * DH, (h + 1) * DH)

    def vcols(h):
        return slice(width + h * DH, width + (h + 1) * DH)

    def plain(slot, first, keys):
        out = []
        for h in range(heads):
            k = kv_ref[pl.ds(first, keys), cols(h)]
            w = silu_weight(contract_lanes(qs[slot][0:ROWS, cols(h)], k)).astype(jnp.bfloat16)
            v = kv_ref[pl.ds(first, keys), vcols(h)]
            out.append(jnp.dot(w, v, preferred_element_type=jnp.float32))
        for h in range(heads):
            acc[:, cols(h)] += out[h]

    for slot in range(NY):
        q_first = ((y + slot) * NZ + z) * ROWS
        acc[...] = jnp.zeros_like(acc)

        def general(slot=slot, q_first=q_first):
            def step(b, carry):
                k_first = strip0 + b * ROWS
                full = jnp.bool_(False)
                some = jnp.bool_(False)
                for s, t in zip(starts, ends):
                    full = full | ((s <= k_first) & (t >= q_first + ROWS))
                    some = some | ((s < k_first + ROWS) & (t > k_first) & (s < q_first + ROWS) & (t > q_first))
                full = full & (k_first < q_first)
                some = some & (k_first <= q_first) & jnp.logical_not(full)

                @pl.when(full)
                def _():
                    plain(slot, pl.multiple_of(b * ROWS, ROWS), ROWS)

                @pl.when(some)
                def _():
                    first = pl.multiple_of(b * ROWS, ROWS)
                    row = q_first + lax.broadcasted_iota(jnp.int32, (ROWS, ROWS), 0)
                    col = k_first + lax.broadcasted_iota(jnp.int32, (ROWS, ROWS), 1)
                    mask = jnp.zeros((ROWS, ROWS), jnp.bool_)
                    for s, t in zip(starts, ends):
                        mask = mask | ((row >= s) & (row < t) & (col >= s))
                    mask = mask & (col <= row)
                    for h in range(heads):
                        k = kv_ref[pl.ds(first, ROWS), cols(h)]
                        w = silu_weight(contract_lanes(qs[slot][0:ROWS, cols(h)], k))
                        w = jnp.where(mask, w, 0.0).astype(jnp.bfloat16)
                        v = kv_ref[pl.ds(first, ROWS), vcols(h)]
                        acc[:, cols(h)] += jnp.dot(w, v, preferred_element_type=jnp.float32)

                return carry

            lax.fori_loop(0, NZ, step, 0)

        if slot == 0:
            general()
            own_ref[0:ROWS, :] = acc[...]
        else:
            valid = y + slot < NY
            whole = jnp.bool_(False)
            for s, t in zip(starts, ends):
                whole = whole | ((s <= strip0) & (t >= q_first + ROWS))

            @pl.when(valid & whole)
            def _(slot=slot):
                def step(b, carry):
                    plain(slot, pl.multiple_of(b * 2 * ROWS, 2 * ROWS), 2 * ROWS)
                    return carry

                lax.fori_loop(0, NZ // 2, step, 0)

            @pl.when(valid & jnp.logical_not(whole))
            def _(general=general):
                general()

            (o1, o2, o3)[slot - 1][0:ROWS, :] = acc[...].astype(jnp.bfloat16)

    lows, highs = [], []
    for slot in range(NY):
        cq[slot * CROWS : (slot + 1) * CROWS, :] = qs[slot][ROWS:QROWS, :]
        first = pl.multiple_of((lax.rem(y + slot, NY) * NZ + z) * CROWS, CROWS)
        user = cu_ref[pl.ds(first, CROWS), :]
        lows.append(jnp.where(user == 0, starts[0], starts[1]))
        highs.append(jnp.where(user == 0, ends[0], ends[1]))
    low = jnp.concatenate(lows, 0)
    high = jnp.concatenate(highs, 0)
    cacc[...] = jnp.zeros_like(cacc)

    def cstep(b, carry):
        first = pl.multiple_of(b * ROWS, ROWS)
        col = strip0 + first + lax.broadcasted_iota(jnp.int32, (NY * CROWS, ROWS), 1)
        mask = (col >= low) & (col < high)
        for h in range(heads):
            k = kv_ref[pl.ds(first, ROWS), cols(h)]
            w = silu_weight(contract_lanes(cq[:, cols(h)], k))
            w = jnp.where(mask, w, 0.0).astype(jnp.bfloat16)
            v = kv_ref[pl.ds(first, ROWS), vcols(h)]
            cacc[:, cols(h)] += jnp.dot(w, v, preferred_element_type=jnp.float32)
        return carry

    lax.fori_loop(0, NZ, cstep, 0)
    own_ref[ROWS:QROWS, :] = cacc[0:CROWS, :]
    for slot in range(1, NY):
        (o1, o2, o3)[slot - 1][ROWS:QROWS, :] = cacc[slot * CROWS : (slot + 1) * CROWS, :].astype(jnp.bfloat16)


def attend(heads, head_block, place, starts, lens, queries, kv, users):
    width = heads * DH
    smem = pl.BlockSpec(memory_space=pltpu.SMEM)
    vmem = pl.BlockSpec(memory_space=pltpu.VMEM)
    q_spec = pl.BlockSpec((QROWS, width), lambda i: (0, head_block))
    whole = lambda shape: pl.BlockSpec(shape, lambda i: (0, 0))
    return pl.pallas_call(
        functools.partial(attend_kernel, heads),
        grid=(1,),
        in_specs=[smem, smem, smem, q_spec, q_spec, q_spec, q_spec, vmem, vmem],
        out_specs=[whole((QROWS, width))] * 4,
        out_shape=[jax.ShapeDtypeStruct((QROWS, width), jnp.float32)]
        + [jax.ShapeDtypeStruct((QROWS, width), jnp.bfloat16)] * 3,
        scratch_shapes=[
            pltpu.VMEM((ROWS, width), jnp.float32),
            pltpu.VMEM((NY * CROWS, width), jnp.bfloat16),
            pltpu.VMEM((NY * CROWS, width), jnp.float32),
        ],
        compiler_params=pltpu.CompilerParams(vmem_limit_bytes=VMEM_LIMIT),
        cost_estimate=pl.CostEstimate(flops=heads * 2 * 2 * QROWS * 4 * STRIP * DH, bytes_accessed=4 << 20, transcendentals=0),
        name="attend",
    )(place, starts, lens, *queries, kv, users)


def finish_kernel(parts, *refs):
    n = parts * 4
    totals = refs[:n]
    hg, hx, cq, ck, cv, cg, cx, w_ref, ho, co = refs[n:]
    sums = []
    for p in range(parts):
        total = totals[4 * p][...]
        for i in range(1, 4):
            total = total + totals[4 * p + i][...].astype(jnp.float32)
        sums.append(total)
    total = sums[0] if parts == 1 else jnp.concatenate(sums, axis=1)
    own = []
    for h in range(HEADS):
        at = slice(h * DH, (h + 1) * DH)
        scores = jnp.sum(cq[:, at].astype(jnp.float32) * ck[:, at].astype(jnp.float32), axis=-1, keepdims=True)
        weight = silu_weight(scores).astype(jnp.bfloat16).astype(jnp.float32)
        own.append(weight * cv[:, at].astype(jnp.float32))

    def tail(rows, gate, inputs, out):
        mean = jnp.mean(rows, axis=-1, keepdims=True)
        centered = rows - mean
        spread = jnp.mean(centered * centered, axis=-1, keepdims=True)
        normed = centered * lax.rsqrt(spread + 1e-05)
        gated = (normed * gate[...].astype(jnp.float32)).astype(jnp.bfloat16)
        mixed = jnp.dot(gated, w_ref[...], preferred_element_type=jnp.float32)
        out[...] = (inputs[...].astype(jnp.float32) + mixed).astype(jnp.bfloat16)

    tail(total[0:ROWS], hg, hx, ho)
    tail(total[ROWS:QROWS] + jnp.concatenate(own, axis=1), cg, cx, co)


def finish(totals, parts, hg, hx, cq, ck, cv, cg, cx, w):
    vmem = pl.BlockSpec(memory_space=pltpu.VMEM)
    return pl.pallas_call(
        functools.partial(finish_kernel, parts),
        in_specs=[vmem] * (len(totals) + 8),
        out_specs=[vmem] * 2,
        out_shape=[jax.ShapeDtypeStruct(hx.shape, jnp.bfloat16), jax.ShapeDtypeStruct(cx.shape, jnp.bfloat16)],
        compiler_params=pltpu.CompilerParams(vmem_limit_bytes=VMEM_LIMIT),
        name="finish",
    )(*totals, hg, hx, cq, ck, cv, cg, cx, w)


def turn(array, axis, count, step):
    return lax.ppermute(array, axis, [(i, (i + step) % count) for i in range(count)])


def on_device(
    hist_query, hist_key, hist_value, hist_gate, hist_input,
    cand_query, cand_key, cand_value, cand_gate, cand_input,
    cand_user, hist_len, hist_start, out_weight,
):
    place = jnp.stack([lax.axis_index("y"), lax.axis_index("z")]).astype(jnp.int32)
    users = cand_user.reshape(-1, 1)
    kv = lax.all_gather(jnp.concatenate([hist_key, hist_value], axis=1), "z", axis=0, tiled=True)
    mine = jnp.concatenate([hist_query, cand_query], axis=0)
    queries = [mine] + [turn(mine, "y", NY, -k) for k in (1, 2, 3)]
    own, *away = attend(HEADS, 0, place, hist_start, hist_len, queries, kv, users)
    back = [turn(a, "y", NY, k) for k, a in zip((1, 2, 3), away)]
    return finish(
        [own] + back, 1, hist_gate, hist_input, cand_query, cand_key, cand_value, cand_gate, cand_input, out_weight
    )


def solution(mesh):
    grid = Mesh(mesh.devices.reshape(-1, NY, NZ), ("batch", "y", "z"))
    rows = P(("batch", "y", "z"), None)
    return jax.shard_map(
        on_device,
        mesh=grid,
        in_specs=(rows,) * 10 + (P("batch"), P("batch"), P("batch"), P()),
        out_specs=(rows, rows),
        check_vma=False,
    )
```

```python
import functools
import math

import jax
import jax.numpy as jnp
from jax import lax
from jax.experimental import pallas as pl
from jax.experimental.pallas import tpu as pltpu
from jax.sharding import Mesh, PartitionSpec as P

HEADS = 4
DH = 128
NY = 4
NZ = 8
ROWS = 256
CROWS = 32
QROWS = ROWS + CROWS
STRIP = NZ * ROWS
BLOCK = 128
HALF_HEADS = 2
WIDTH = HALF_HEADS * DH
CKEYS = 1024
HALF = 1.0 / (2.0 * math.sqrt(DH))
VMEM_LIMIT = 48 * 1024 * 1024


def contract_lanes(a, b):
    return lax.dot_general(a, b, (((1,), (1,)), ((), ())), preferred_element_type=jnp.float32)


def silu_weight(scores):
    half = scores * HALF
    return half * jnp.tanh(half) + half


def attend_kernel(pieces, place_ref, start_ref, len_ref, q0, q1, q2, q3, cu_ref, *refs):
    kv_refs = refs[:pieces]
    own_ref, o1, o2, o3, kv, qs, acc, cq, cacc = refs[pieces:]
    y = place_ref[0]
    z = place_ref[1]
    starts = [start_ref[u] for u in range(2)]
    ends = [start_ref[u] + len_ref[u] for u in range(2)]
    strip0 = y * STRIP

    def kcols(h):
        return slice(h * DH, (h + 1) * DH)

    def vcols(h):
        return slice(WIDTH + h * DH, WIDTH + (h + 1) * DH)

    if pieces == 1:
        kv = kv_refs[0]
    else:
        for piece, ref in enumerate(kv_refs):
            block = lax.rem(z + piece, NZ)
            kv[pl.ds(pl.multiple_of(block * ROWS, ROWS), ROWS), :] = ref[...]
    for slot, ref in enumerate((q0, q1, q2, q3)):
        qs[slot * ROWS : (slot + 1) * ROWS, :] = ref[0:ROWS, :]
        cq[slot * CROWS : (slot + 1) * CROWS, :] = ref[ROWS:QROWS, :]
    acc[...] = jnp.zeros_like(acc)

    def body(row, rows, first, keys, triangle=False):
        mask = None
        if triangle:
            mask = lax.broadcasted_iota(jnp.int32, (rows, keys), 0) >= lax.broadcasted_iota(jnp.int32, (rows, keys), 1)
        out = []
        for h in range(HALF_HEADS):
            w = silu_weight(contract_lanes(qs[pl.ds(row, rows), kcols(h)], kv[pl.ds(first, keys), kcols(h)]))
            if triangle:
                w = jnp.where(mask, w, 0.0)
            out.append(jnp.dot(w.astype(jnp.bfloat16), kv[pl.ds(first, keys), vcols(h)], preferred_element_type=jnp.float32))
        for h in range(HALF_HEADS):
            acc[pl.ds(row, rows), kcols(h)] += out[h]

    def run(row, rows, low, count):
        count = jnp.maximum(count, 0)
        wide = count // 8

        def step(i, carry):
            body(row, rows, pl.multiple_of((low + 8 * i) * BLOCK, BLOCK), 8 * BLOCK)
            return carry

        lax.fori_loop(0, wide, step, 0)
        done = low + 8 * wide
        for size in (4, 2, 1):
            here = (count // size) % 2 == 1

            @pl.when(here)
            def _(done=done, size=size):
                body(row, rows, pl.multiple_of(done * BLOCK, BLOCK), size * BLOCK)

            done = done + jnp.where(here, size, 0)

    def owner_of(event):
        low, end = jnp.int32(-1), jnp.int32(-1)
        for s, t in zip(starts, ends):
            inside = (s <= event) & (event < t)
            low = jnp.where(inside, s, low)
            end = jnp.where(inside, t, end)
        return low, end

    def slot_step(slot, carry):
        event = ((y + slot) * NZ + z) * ROWS
        row = pl.multiple_of(slot * ROWS, ROWS)
        low0, _ = owner_of(event)
        low1, _ = owner_of(event + BLOCK)
        near = slot == 0
        same = (low0 == low1) & (low0 >= 0)
        top = jnp.where(near, 2 * z, NZ * ROWS // BLOCK)

        @pl.when(same)
        def _():
            low = jnp.maximum(low0 - strip0, 0) // BLOCK
            run(row, ROWS, low, top - low)

            @pl.when(near)
            def _():
                body(row, ROWS, pl.multiple_of(z * ROWS, ROWS), ROWS, triangle=True)

        @pl.when(jnp.logical_not(same))
        def _():
            def half_step(half, carry):
                start = jnp.where(half == 0, low0, low1)

                @pl.when(start >= 0)
                def _():
                    low = jnp.maximum(start - strip0, 0) // BLOCK
                    upto = jnp.where(near, 2 * z + half, top)
                    at = pl.multiple_of(row + half * BLOCK, BLOCK)
                    run(at, BLOCK, low, upto - low)

                    @pl.when(near)
                    def _():
                        body(at, BLOCK, pl.multiple_of((2 * z + half) * BLOCK, BLOCK), BLOCK, triangle=True)

                return carry

            lax.fori_loop(0, 2, half_step, 0)

        return carry

    lax.fori_loop(0, NY - y, slot_step, 0)

    for slot in range(NY):
        event = ((y + slot) * NZ + z) * ROWS
        _, end0 = owner_of(event)
        _, end1 = owner_of(event + BLOCK)
        at = lax.broadcasted_iota(jnp.int32, (ROWS, WIDTH), 0)
        end = jnp.where(at < BLOCK, end0, end1)
        rows = jnp.where(event + at < end, acc[slot * ROWS : (slot + 1) * ROWS, :], 0.0)
        if slot == 0:
            own_ref[0:ROWS, :] = rows
        else:
            (o1, o2, o3)[slot - 1][0:ROWS, :] = rows.astype(jnp.bfloat16)

    lows, highs = [], []
    for slot in range(NY):
        first = pl.multiple_of((lax.rem(y + slot, NY) * NZ + z) * CROWS, CROWS)
        user = cu_ref[pl.ds(first, CROWS), :]
        lows.append(jnp.where(user == 0, starts[0], starts[1]) - strip0)
        highs.append(jnp.where(user == 0, ends[0], ends[1]) - strip0)
    low = jnp.concatenate(lows, 0)
    high = jnp.concatenate(highs, 0)
    cacc[...] = jnp.zeros_like(cacc)

    def cand_step(i, carry):
        first = pl.multiple_of(i * CKEYS, CKEYS)
        col = first + lax.broadcasted_iota(jnp.int32, (NY * CROWS, CKEYS), 1)
        mask = (col >= low) & (col < high)
        out = []
        for h in range(HALF_HEADS):
            w = silu_weight(contract_lanes(cq[:, kcols(h)], kv[pl.ds(first, CKEYS), kcols(h)]))
            w = jnp.where(mask, w, 0.0).astype(jnp.bfloat16)
            out.append(jnp.dot(w, kv[pl.ds(first, CKEYS), vcols(h)], preferred_element_type=jnp.float32))
        for h in range(HALF_HEADS):
            cacc[:, kcols(h)] += out[h]
        return carry

    lax.fori_loop(0, STRIP // CKEYS, cand_step, 0)
    own_ref[ROWS:QROWS, :] = cacc[0:CROWS, :]
    for slot in range(1, NY):
        (o1, o2, o3)[slot - 1][ROWS:QROWS, :] = cacc[slot * CROWS : (slot + 1) * CROWS, :].astype(jnp.bfloat16)


def attend(part, place, starts, lens, queries, pieces, users):
    smem = pl.BlockSpec(memory_space=pltpu.SMEM)
    vmem = pl.BlockSpec(memory_space=pltpu.VMEM)
    q_spec = pl.BlockSpec((QROWS, WIDTH), lambda i: (0, part))
    o_spec = pl.BlockSpec((QROWS, WIDTH), lambda i: (0, 0))
    return pl.pallas_call(
        functools.partial(attend_kernel, len(pieces)),
        grid=(1,),
        in_specs=[smem, smem, smem, q_spec, q_spec, q_spec, q_spec] + [vmem] * (1 + len(pieces)),
        out_specs=[o_spec] * 4,
        out_shape=[jax.ShapeDtypeStruct((QROWS, WIDTH), jnp.float32)]
        + [jax.ShapeDtypeStruct((QROWS, WIDTH), jnp.bfloat16)] * 3,
        scratch_shapes=[
            pltpu.VMEM((STRIP if len(pieces) > 1 else 16, 2 * WIDTH), jnp.bfloat16),
            pltpu.VMEM((NY * ROWS, WIDTH), jnp.bfloat16),
            pltpu.VMEM((NY * ROWS, WIDTH), jnp.float32),
            pltpu.VMEM((NY * CROWS, WIDTH), jnp.bfloat16),
            pltpu.VMEM((NY * CROWS, WIDTH), jnp.float32),
        ],
        compiler_params=pltpu.CompilerParams(vmem_limit_bytes=VMEM_LIMIT),
        cost_estimate=pl.CostEstimate(
            flops=2 * HALF_HEADS * 2 * QROWS * 4 * STRIP * DH, bytes_accessed=4 << 20, transcendentals=0
        ),
        name="attend",
    )(place, starts, lens, *queries, users, *pieces)


def finish_kernel(parts, *refs):
    n = parts * 4
    totals = refs[:n]
    hg, hx, cq, ck, cv, cg, cx, w_ref, ho, co = refs[n:]
    sums = []
    for p in range(parts):
        total = totals[4 * p][...]
        for i in range(1, 4):
            total = total + totals[4 * p + i][...].astype(jnp.float32)
        sums.append(total)
    total = sums[0] if parts == 1 else jnp.concatenate(sums, axis=1)
    own = []
    for h in range(HEADS):
        at = slice(h * DH, (h + 1) * DH)
        scores = jnp.sum(cq[:, at].astype(jnp.float32) * ck[:, at].astype(jnp.float32), axis=-1, keepdims=True)
        weight = silu_weight(scores).astype(jnp.bfloat16).astype(jnp.float32)
        own.append(weight * cv[:, at].astype(jnp.float32))

    def tail(rows, gate, inputs, out):
        mean = jnp.mean(rows, axis=-1, keepdims=True)
        centered = rows - mean
        spread = jnp.mean(centered * centered, axis=-1, keepdims=True)
        normed = centered * lax.rsqrt(spread + 1e-05)
        gated = (normed * gate[...].astype(jnp.float32)).astype(jnp.bfloat16)
        mixed = jnp.dot(gated, w_ref[...], preferred_element_type=jnp.float32)
        out[...] = (inputs[...].astype(jnp.float32) + mixed).astype(jnp.bfloat16)

    tail(total[0:ROWS], hg, hx, ho)
    tail(total[ROWS:QROWS] + jnp.concatenate(own, axis=1), cg, cx, co)


def finish(totals, parts, hg, hx, cq, ck, cv, cg, cx, w):
    vmem = pl.BlockSpec(memory_space=pltpu.VMEM)
    return pl.pallas_call(
        functools.partial(finish_kernel, parts),
        in_specs=[vmem] * (len(totals) + 8),
        out_specs=[vmem] * 2,
        out_shape=[jax.ShapeDtypeStruct(hx.shape, jnp.bfloat16), jax.ShapeDtypeStruct(cx.shape, jnp.bfloat16)],
        compiler_params=pltpu.CompilerParams(vmem_limit_bytes=VMEM_LIMIT),
        name="finish",
    )(*totals, hg, hx, cq, ck, cv, cg, cx, w)


def turn(array, axis, count, step):
    return lax.ppermute(array, axis, [(i, (i + step) % count) for i in range(count)])


def on_device(
    hist_query, hist_key, hist_value, hist_gate, hist_input,
    cand_query, cand_key, cand_value, cand_gate, cand_input,
    cand_user, hist_len, hist_start, out_weight,
):
    place = jnp.stack([lax.axis_index("y"), lax.axis_index("z")]).astype(jnp.int32)
    users = cand_user.reshape(-1, 1)
    left = jnp.concatenate([hist_key[:, :WIDTH], hist_value[:, :WIDTH]], axis=1)
    right = jnp.concatenate([hist_key[:, WIDTH:], hist_value[:, WIDTH:]], axis=1)
    strip = lax.all_gather(right, "z", axis=0, tiled=True)
    up, down = [left], [left]
    for _ in range(3):
        up.append(turn(up[-1], "z", NZ, 1))
        down.append(turn(down[-1], "z", NZ, -1))
    across = turn(up[-1], "z", NZ, 1)
    blocks = down + [across] + up[:0:-1]
    mine = jnp.concatenate([hist_query, cand_query], axis=0)
    queries = [mine] + [turn(mine, "y", NY, -k) for k in (1, 2, 3)]
    totals = []
    for part, pieces in enumerate((blocks, [strip])):
        own, *away = attend(part, place, hist_start, hist_len, queries, pieces, users)
        totals += [own] + [turn(a, "y", NY, k) for k, a in zip((1, 2, 3), away)]
    return finish(
        totals, 2, hist_gate, hist_input, cand_query, cand_key, cand_value, cand_gate, cand_input, out_weight
    )


def solution(mesh):
    grid = Mesh(mesh.devices.reshape(-1, NY, NZ), ("batch", "y", "z"))
    rows = P(("batch", "y", "z"), None)
    return jax.shard_map(
        on_device,
        mesh=grid,
        in_specs=(rows,) * 10 + (P("batch"), P("batch"), P("batch"), P()),
        out_specs=(rows, rows),
        check_vma=False,
    )
```

```python
import functools
import math

import jax
import jax.numpy as jnp
from jax import lax
from jax.experimental import pallas as pl
from jax.experimental.pallas import tpu as pltpu
from jax.sharding import Mesh, PartitionSpec as P

HEADS = 4
DH = 128
NY = 4
NZ = 8
ROWS = 256
CROWS = 32
QROWS = ROWS + CROWS
FOLD = QROWS // 2
REST = ROWS - FOLD
BLOCK = 128
KEYS = NY * ROWS
TOTAL = KEYS + NY * CROWS
NOBODY = 1 << 30
HALF = 1.0 / (2.0 * math.sqrt(DH))
VMEM_LIMIT = 60 * 1024 * 1024
VMEM = pl.BlockSpec(memory_space=pltpu.VMEM)
SMEM = pl.BlockSpec(memory_space=pltpu.SMEM)
PARAMS = pltpu.CompilerParams(vmem_limit_bytes=VMEM_LIMIT)


def contract_lanes(a, b):
    return lax.dot_general(a, b, (((1,), (1,)), ((), ())), preferred_element_type=jnp.float32)


def silu_weight(scores):
    half = scores * HALF
    return (half * jnp.tanh(half) + half).astype(jnp.bfloat16)


def split_kernel(k_ref, v_ref, kv_ref):
    for h in range(HEADS):
        at = slice(h * DH, (h + 1) * DH)
        kv_ref[h * ROWS : (h + 1) * ROWS, 0:DH] = k_ref[:, at]
        kv_ref[h * ROWS : (h + 1) * ROWS, DH : 2 * DH] = v_ref[:, at]


def fold_kernel(q_ref, c_ref, out_ref):
    for h in range(HEADS):
        at = slice(h * DH, (h + 1) * DH)
        out_ref[h * FOLD : (h + 1) * FOLD, 0:DH] = q_ref[0:FOLD, at]
        out_ref[h * FOLD : h * FOLD + REST, DH : 2 * DH] = q_ref[FOLD:ROWS, at]
        out_ref[h * FOLD + REST : (h + 1) * FOLD, DH : 2 * DH] = c_ref[:, at]


def attend_kernel(offsets, first, last, place_ref, start_ref, len_ref, q_ref, user_ref, *refs):
    blocks = 2 if last else len(offsets)
    kv_refs = refs[:blocks]
    refs = refs[blocks:]
    if not first:
        in_ref, *refs = refs
    out_ref, kv, qs, acc = refs
    z = place_ref[1]
    starts = [start_ref[u] for u in range(2)]
    ends = [start_ref[u] + len_ref[u] for u in range(2)]

    size = kv_refs[0].shape[0]
    for i, ref in enumerate(kv_refs):
        kv[i * size : (i + 1) * size, :] = ref[...]
    for s in range(NY):
        qs[s * ROWS : s * ROWS + FOLD, :] = q_ref[s * FOLD : (s + 1) * FOLD, 0:DH]
        qs[s * ROWS + FOLD : (s + 1) * ROWS, :] = q_ref[s * FOLD : s * FOLD + REST, DH : 2 * DH]
        qs[KEYS + s * CROWS : KEYS + (s + 1) * CROWS, :] = q_ref[s * FOLD + REST : (s + 1) * FOLD, DH : 2 * DH]
    if first:
        acc[...] = jnp.zeros_like(acc)
    else:
        acc[...] = in_ref[...]

    lows, stops = [], []
    for half in range(2 * NY):
        event = (half // 2 * NZ + z) * ROWS + half % 2 * BLOCK
        low, stop = jnp.int32(NOBODY), jnp.int32(0)
        for s, t in zip(starts, ends):
            inside = (s <= event) & (event < t)
            low = jnp.where(inside, s, low)
            stop = jnp.where(inside, t, stop)
        lows.append(low)
        stops.append(stop)
    user = user_ref[...]
    cand_low = jnp.where(user == 0, starts[0], starts[1])
    cand_stop = jnp.where(user == 0, ends[0], ends[1])
    column = lax.broadcasted_iota(jnp.int32, (1, ROWS), 1)

    def block_step(part, slots):
        block = z + offsets[-1]
        for n, offset in enumerate(offsets[:-1]):
            block = jnp.where(part == n, z + offset, block)
        block = lax.rem(block, NZ)
        for strip, slot in enumerate(slots):
            row = slot * ROWS
            key = pl.multiple_of(part * KEYS + strip * ROWS, ROWS)
            events = (strip * NZ + block) * ROWS + column
            w = silu_weight(contract_lanes(qs[row:TOTAL, :], kv[pl.ds(key, ROWS), 0:DH]))
            parts = []
            for half in range(2 * slot, 2 * NY):
                at = half * BLOCK - row
                keep = jnp.where(events >= lows[half], 1.0, 0.0).astype(jnp.bfloat16)
                parts.append(w[at : at + BLOCK] * keep)
            keep = jnp.where((events >= cand_low) & (events < cand_stop), 1.0, 0.0).astype(jnp.bfloat16)
            parts.append(w[KEYS - row :] * keep)
            w = parts[0] if len(parts) == 1 else jnp.concatenate(parts, axis=0)
            acc[row:TOTAL, :] += jnp.dot(w, kv[pl.ds(key, ROWS), DH : 2 * DH], preferred_element_type=jnp.float32)

    def step(part, carry):
        block = z + offsets[-1]
        for n, offset in enumerate(offsets[:-1]):
            block = jnp.where(part == n, z + offset, block)
        before = lax.rem(block, NZ) < z

        @pl.when(before)
        def _():
            block_step(part, range(0, NY))

        @pl.when(jnp.logical_not(before))
        def _():
            block_step(part, range(1, NY + 1))

        return carry

    lax.fori_loop(0, len(offsets), step, 0)

    if offsets[0] == 0:
        at = lax.broadcasted_iota(jnp.int32, (BLOCK, ROWS), 0)
        to = lax.broadcasted_iota(jnp.int32, (BLOCK, ROWS), 1)
        for s in range(NY):
            rows = slice(s * ROWS, (s + 1) * ROWS)
            w = silu_weight(contract_lanes(qs[rows, :], kv[rows, 0:DH]))
            event = (s * NZ + z) * ROWS
            parts = []
            for half in range(2):
                mask = (to <= at + half * BLOCK) & (event + to >= lows[2 * s + half])
                parts.append(w[half * BLOCK : (half + 1) * BLOCK] * jnp.where(mask, 1.0, 0.0).astype(jnp.bfloat16))
            w = jnp.concatenate(parts, axis=0)
            acc[rows, :] += jnp.dot(w, kv[rows, DH : 2 * DH], preferred_element_type=jnp.float32)

    if not last:
        out_ref[...] = acc[...]
    else:
        for s in range(NY):
            event = (s * NZ + z) * ROWS
            at = lax.broadcasted_iota(jnp.int32, (ROWS, DH), 0)
            stop = jnp.where(at < BLOCK, stops[2 * s], stops[2 * s + 1])
            rows = jnp.where(event + at < stop, acc[s * ROWS : (s + 1) * ROWS, :], 0.0).astype(jnp.bfloat16)
            out_ref[s * FOLD : (s + 1) * FOLD, 0:DH] = rows[0:FOLD]
            out_ref[s * FOLD : s * FOLD + REST, DH : 2 * DH] = rows[FOLD:ROWS]
            cands = acc[KEYS + s * CROWS : KEYS + (s + 1) * CROWS, :].astype(jnp.bfloat16)
            out_ref[s * FOLD + REST : (s + 1) * FOLD, DH : 2 * DH] = cands


def attend(offsets, where, queries, users, blocks, total, last):
    first = total is None
    shape = jax.ShapeDtypeStruct((NY * FOLD, 2 * DH), jnp.bfloat16) if last else jax.ShapeDtypeStruct((TOTAL, DH), jnp.float32)
    state = [] if first else [total]
    return pl.pallas_call(
        functools.partial(attend_kernel, offsets, first, last),
        in_specs=[SMEM] * 3 + [VMEM] * (2 + len(blocks) + len(state)),
        out_specs=VMEM,
        out_shape=shape,
        scratch_shapes=[
            pltpu.VMEM((len(offsets) * KEYS, 2 * DH), jnp.bfloat16),
            pltpu.VMEM((TOTAL, DH), jnp.bfloat16),
            pltpu.VMEM((TOTAL, DH), jnp.float32),
        ],
        compiler_params=PARAMS,
        cost_estimate=pl.CostEstimate(
            flops=len(offsets) * 4 * TOTAL * KEYS * DH, bytes_accessed=len(offsets) << 20, transcendentals=0
        ),
        name="attend",
    )(*where, queries, users, *blocks, *state)


def finish_kernel(t_ref, hg, hx, cq, ck, cv, cg, cx, w_ref, ho, co):
    hist, cand = [], []
    for h in range(HEADS):
        at = slice(h * DH, (h + 1) * DH)
        rows = t_ref[h * FOLD : (h + 1) * FOLD, :].astype(jnp.float32)
        hist.append(jnp.concatenate([rows[:, 0:DH], rows[0:REST, DH : 2 * DH]], axis=0))
        scores = jnp.sum(cq[:, at].astype(jnp.float32) * ck[:, at].astype(jnp.float32), axis=-1, keepdims=True)
        weight = silu_weight(scores).astype(jnp.float32)
        cand.append(rows[REST:FOLD, DH : 2 * DH] + weight * cv[:, at].astype(jnp.float32))

    def tail(total, gate, inputs, out):
        mean = jnp.mean(total, axis=-1, keepdims=True)
        centered = total - mean
        spread = jnp.mean(centered * centered, axis=-1, keepdims=True)
        normed = centered * lax.rsqrt(spread + 1e-05)
        gated = (normed * gate[...].astype(jnp.float32)).astype(jnp.bfloat16)
        mixed = jnp.dot(gated, w_ref[...], preferred_element_type=jnp.float32)
        out[...] = (inputs[...].astype(jnp.float32) + mixed).astype(jnp.bfloat16)

    tail(jnp.concatenate(hist, axis=1), hg, hx, ho)
    tail(jnp.concatenate(cand, axis=1), cg, cx, co)


def call(kernel, shapes, *args):
    return pl.pallas_call(
        kernel,
        in_specs=[VMEM] * len(args),
        out_specs=[VMEM] * len(shapes),
        out_shape=[jax.ShapeDtypeStruct(s, jnp.bfloat16) for s in shapes],
        compiler_params=PARAMS,
    )(*args)


def turn(array, step):
    return lax.ppermute(array, "z", [(i, (i + step) % NZ) for i in range(NZ)])


def spread(array):
    return lax.all_to_all(array, "y", 0, 0, tiled=True)


def on_device(
    hist_query, hist_key, hist_value, hist_gate, hist_input,
    cand_query, cand_key, cand_value, cand_gate, cand_input,
    cand_user, hist_len, hist_start, out_weight,
):
    z = lax.axis_index("z")
    where = (jnp.stack([lax.axis_index("y"), z]).astype(jnp.int32), hist_start, hist_len)
    users = lax.dynamic_index_in_dim(cand_user.reshape(NY, NZ, CROWS), z, axis=1).reshape(NY * CROWS, 1)
    (own,) = call(split_kernel, [(KEYS, 2 * DH)], hist_key, hist_value)
    own = spread(own)
    (folded,) = call(fold_kernel, [(HEADS * FOLD, 2 * DH)], hist_query, cand_query)
    up1, down1 = turn(own, 1), turn(own, -1)
    queries = spread(folded)
    up1, down1, queries = lax.optimization_barrier((up1, down1, queries))
    up2, down2 = turn(up1, 1), turn(down1, -1)
    total = attend((0, 7, 1), where, queries, users, (own, up1, down1), None, False)
    up2, down2, total = lax.optimization_barrier((up2, down2, total))
    up3, down3 = turn(up2, 1), turn(down2, -1)
    total = attend((6, 2), where, queries, users, (up2, down2), total, False)
    up3, down3, total = lax.optimization_barrier((up3, down3, total))
    low, high = turn(up3[: KEYS // 2], 1), turn(down3[KEYS // 2 :], -1)
    total = attend((5, 3), where, queries, users, (up3, down3), total, False)
    total = attend((4,), where, queries, users, (low, high), total, True)
    return tuple(
        call(
            finish_kernel, [hist_input.shape, cand_input.shape],
            spread(total), hist_gate, hist_input, cand_query, cand_key, cand_value, cand_gate, cand_input, out_weight,
        )
    )


def solution(mesh):
    grid = Mesh(mesh.devices.reshape(-1, NY, NZ), ("batch", "y", "z"))
    rows = P(("batch", "y", "z"), None)
    return jax.shard_map(
        on_device,
        mesh=grid,
        in_specs=(rows,) * 10 + (P("batch"), P("batch"), P("batch"), P()),
        out_specs=(rows, rows),
        check_vma=False,
    )
```

```python
import functools
import math

import jax
import jax.numpy as jnp
from jax import lax
from jax.experimental import pallas as pl
from jax.experimental.pallas import tpu as pltpu
from jax.sharding import Mesh, PartitionSpec as P

HEADS = 4
DH = 128
NY = 4
NZ = 8
ROWS = 256
CROWS = 32
QROWS = ROWS + CROWS
FOLD = QROWS // 2
REST = ROWS - FOLD
PART = ROWS + FOLD
BLOCK = 128
KEYS = NY * ROWS
TOTAL = KEYS + NY * CROWS
NOBODY = 1 << 30
HALF = 1.0 / (2.0 * math.sqrt(DH))
VMEM_LIMIT = 16 * 1024 * 1024
VMEM = pl.BlockSpec(memory_space=pltpu.VMEM)
SMEM = pl.BlockSpec(memory_space=pltpu.SMEM)
PARAMS = pltpu.CompilerParams(vmem_limit_bytes=VMEM_LIMIT)


def contract_lanes(a, b):
    return lax.dot_general(a, b, (((1,), (1,)), ((), ())), preferred_element_type=jnp.float32)


def silu_weight(scores):
    half = scores * HALF
    return (half * jnp.tanh(half) + half).astype(jnp.bfloat16)


def split_kernel(k_ref, v_ref, q_ref, c_ref, out_ref):
    for h in range(HEADS):
        at = slice(h * DH, (h + 1) * DH)
        row = h * PART
        out_ref[row : row + ROWS, 0:DH] = k_ref[:, at]
        out_ref[row : row + ROWS, DH : 2 * DH] = v_ref[:, at]
        row += ROWS
        out_ref[row : row + FOLD, 0:DH] = q_ref[0:FOLD, at]
        out_ref[row : row + REST, DH : 2 * DH] = q_ref[FOLD:ROWS, at]
        out_ref[row + REST : row + FOLD, DH : 2 * DH] = c_ref[:, at]


def attend_kernel(offsets, first, last, place_ref, start_ref, len_ref, q_ref, user_ref, *refs):
    blocks = 2 if last else len(offsets)
    kv_refs = refs[:blocks]
    refs = refs[blocks:]
    if not first:
        in_ref, *refs = refs
    out_ref, kv, qs, acc = refs
    z = place_ref[0]
    starts = [start_ref[u] for u in range(2)]
    ends = [start_ref[u] + len_ref[u] for u in range(2)]

    size = kv_refs[0].shape[0]
    for i, ref in enumerate(kv_refs):
        kv[i * size : (i + 1) * size, :] = ref[...]
    for s in range(NY):
        row = s * PART + ROWS
        qs[s * ROWS : s * ROWS + FOLD, :] = q_ref[row : row + FOLD, 0:DH]
        qs[s * ROWS + FOLD : (s + 1) * ROWS, :] = q_ref[row : row + REST, DH : 2 * DH]
        qs[KEYS + s * CROWS : KEYS + (s + 1) * CROWS, :] = q_ref[row + REST : row + FOLD, DH : 2 * DH]
    if first:
        acc[...] = jnp.zeros_like(acc)
    else:
        acc[...] = in_ref[...]

    lows, stops = [], []
    for half in range(2 * NY):
        event = (half // 2 * NZ + z) * ROWS + half % 2 * BLOCK
        low, stop = jnp.int32(NOBODY), jnp.int32(0)
        for s, t in zip(starts, ends):
            inside = (s <= event) & (event < t)
            low = jnp.where(inside, s, low)
            stop = jnp.where(inside, t, stop)
        lows.append(low)
        stops.append(stop)
    user = user_ref[...]
    cand_low = jnp.where(user == 0, starts[0], starts[1])
    cand_stop = jnp.where(user == 0, ends[0], ends[1])
    column = lax.broadcasted_iota(jnp.int32, (1, ROWS), 1)

    def block_step(part, slots):
        block = z + offsets[-1]
        for n, offset in enumerate(offsets[:-1]):
            block = jnp.where(part == n, z + offset, block)
        block = lax.rem(block, NZ)
        for strip, slot in enumerate(slots):
            row = slot * ROWS
            key = pl.multiple_of(part * KEYS + strip * ROWS, ROWS)
            events = (strip * NZ + block) * ROWS + column
            w = silu_weight(contract_lanes(qs[row:TOTAL, :], kv[pl.ds(key, ROWS), 0:DH]))
            parts = []
            for half in range(2 * slot, 2 * NY):
                at = half * BLOCK - row
                keep = jnp.where(events >= lows[half], 1.0, 0.0).astype(jnp.bfloat16)
                parts.append(w[at : at + BLOCK] * keep)
            keep = jnp.where((events >= cand_low) & (events < cand_stop), 1.0, 0.0).astype(jnp.bfloat16)
            parts.append(w[KEYS - row :] * keep)
            w = parts[0] if len(parts) == 1 else jnp.concatenate(parts, axis=0)
            acc[row:TOTAL, :] += jnp.dot(w, kv[pl.ds(key, ROWS), DH : 2 * DH], preferred_element_type=jnp.float32)

    def step(part, carry):
        block = z + offsets[-1]
        for n, offset in enumerate(offsets[:-1]):
            block = jnp.where(part == n, z + offset, block)
        before = lax.rem(block, NZ) < z

        @pl.when(before)
        def _():
            block_step(part, range(0, NY))

        @pl.when(jnp.logical_not(before))
        def _():
            block_step(part, range(1, NY + 1))

        return carry

    lax.fori_loop(0, len(offsets), step, 0)

    if first:
        at = lax.broadcasted_iota(jnp.int32, (BLOCK, ROWS), 0)
        to = lax.broadcasted_iota(jnp.int32, (BLOCK, ROWS), 1)
        for s in range(NY):
            rows = slice(s * ROWS, (s + 1) * ROWS)
            w = silu_weight(contract_lanes(qs[rows, :], kv[rows, 0:DH]))
            event = (s * NZ + z) * ROWS
            parts = []
            for half in range(2):
                mask = (to <= at + half * BLOCK) & (event + to >= lows[2 * s + half])
                parts.append(w[half * BLOCK : (half + 1) * BLOCK] * jnp.where(mask, 1.0, 0.0).astype(jnp.bfloat16))
            w = jnp.concatenate(parts, axis=0)
            acc[rows, :] += jnp.dot(w, kv[rows, DH : 2 * DH], preferred_element_type=jnp.float32)

    if not last:
        out_ref[...] = acc[...]
    else:
        for s in range(NY):
            event = (s * NZ + z) * ROWS
            at = lax.broadcasted_iota(jnp.int32, (ROWS, DH), 0)
            stop = jnp.where(at < BLOCK, stops[2 * s], stops[2 * s + 1])
            rows = jnp.where(event + at < stop, acc[s * ROWS : (s + 1) * ROWS, :], 0.0).astype(jnp.bfloat16)
            out_ref[s * FOLD : (s + 1) * FOLD, 0:DH] = rows[0:FOLD]
            out_ref[s * FOLD : s * FOLD + REST, DH : 2 * DH] = rows[FOLD:ROWS]
            cands = acc[KEYS + s * CROWS : KEYS + (s + 1) * CROWS, :].astype(jnp.bfloat16)
            out_ref[s * FOLD + REST : (s + 1) * FOLD, DH : 2 * DH] = cands


def attend(offsets, where, queries, users, blocks, total, last):
    first = total is None
    shape = jax.ShapeDtypeStruct((NY * FOLD, 2 * DH), jnp.bfloat16) if last else jax.ShapeDtypeStruct((TOTAL, DH), jnp.float32)
    state = [] if first else [total]
    return pl.pallas_call(
        functools.partial(attend_kernel, offsets, first, last),
        in_specs=[SMEM] * 3 + [VMEM] * (2 + len(blocks) + len(state)),
        out_specs=VMEM,
        out_shape=shape,
        scratch_shapes=[
            pltpu.VMEM((len(offsets) * KEYS, 2 * DH), jnp.bfloat16),
            pltpu.VMEM((TOTAL, DH), jnp.bfloat16),
            pltpu.VMEM((TOTAL, DH), jnp.float32),
        ],
        compiler_params=PARAMS,
        cost_estimate=pl.CostEstimate(
            flops=len(offsets) * 4 * TOTAL * KEYS * DH, bytes_accessed=len(offsets) << 20, transcendentals=0
        ),
        name="attend",
    )(*where, queries, users, *blocks, *state)


def finish_kernel(t_ref, hg, hx, cq, ck, cv, cg, cx, w_ref, ho, co):
    hist, cand = [], []
    for h in range(HEADS):
        at = slice(h * DH, (h + 1) * DH)
        rows = t_ref[h * FOLD : (h + 1) * FOLD, :].astype(jnp.float32)
        hist.append(jnp.concatenate([rows[:, 0:DH], rows[0:REST, DH : 2 * DH]], axis=0))
        scores = jnp.sum(cq[:, at].astype(jnp.float32) * ck[:, at].astype(jnp.float32), axis=-1, keepdims=True)
        weight = silu_weight(scores).astype(jnp.float32)
        cand.append(rows[REST:FOLD, DH : 2 * DH] + weight * cv[:, at].astype(jnp.float32))

    def tail(total, gate, inputs, out):
        mean = jnp.mean(total, axis=-1, keepdims=True)
        centered = total - mean
        spread = jnp.mean(centered * centered, axis=-1, keepdims=True)
        normed = centered * lax.rsqrt(spread + 1e-05)
        gated = (normed * gate[...].astype(jnp.float32)).astype(jnp.bfloat16)
        mixed = jnp.dot(gated, w_ref[...], preferred_element_type=jnp.float32)
        out[...] = (inputs[...].astype(jnp.float32) + mixed).astype(jnp.bfloat16)

    tail(jnp.concatenate(hist, axis=1), hg, hx, ho)
    tail(jnp.concatenate(cand, axis=1), cg, cx, co)


def call(kernel, shapes, *args):
    return pl.pallas_call(
        kernel,
        in_specs=[VMEM] * len(args),
        out_specs=[VMEM] * len(shapes),
        out_shape=[jax.ShapeDtypeStruct(s, jnp.bfloat16) for s in shapes],
        compiler_params=PARAMS,
    )(*args)


def turn(array, step):
    return lax.ppermute(array, "z", [(i, (i + step) % NZ) for i in range(NZ)])


def spread(array):
    return lax.all_to_all(array, "y", 0, 0, tiled=True)


def on_device(
    hist_query, hist_key, hist_value, hist_gate, hist_input,
    cand_query, cand_key, cand_value, cand_gate, cand_input,
    cand_user, hist_len, hist_start, out_weight,
):
    z = lax.axis_index("z")
    where = (z.astype(jnp.int32).reshape(1), hist_start, hist_len)
    users = lax.dynamic_index_in_dim(cand_user.reshape(NY, NZ, CROWS), z, axis=1).reshape(NY * CROWS, 1)
    (parts,) = call(split_kernel, [(HEADS * PART, 2 * DH)], hist_key, hist_value, hist_query, cand_query)
    queries = spread(parts)
    own = queries.reshape(NY, PART, 2 * DH)[:, :ROWS].reshape(KEYS, 2 * DH)
    up, down = turn(own, 1), turn(own, -1)
    total = attend((0,), where, queries, users, (own,), None, False)
    for step in (1, 2):
        up, held = lax.optimization_barrier((up, total))
        down, total = lax.optimization_barrier((down, held))
        blocks = (up, down)
        up, down = turn(up, 1), turn(down, -1)
        total = attend((NZ - step, step), where, queries, users, blocks, total, False)
    up, held = lax.optimization_barrier((up, total))
    down, total = lax.optimization_barrier((down, held))
    low, high = turn(up[: KEYS // 2], 1), turn(down[KEYS // 2 :], -1)
    total = attend((NZ - 3, 3), where, queries, users, (up, down), total, False)
    total = attend((4,), where, queries, users, (low, high), total, True)
    return tuple(
        call(
            finish_kernel, [hist_input.shape, cand_input.shape],
            spread(total), hist_gate, hist_input, cand_query, cand_key, cand_value, cand_gate, cand_input, out_weight,
        )
    )


def solution(mesh):
    grid = Mesh(mesh.devices.reshape(-1, NY, NZ), ("batch", "y", "z"))
    rows = P(("batch", "y", "z"), None)
    return jax.shard_map(
        on_device,
        mesh=grid,
        in_specs=(rows,) * 10 + (P("batch"), P("batch"), P("batch"), P()),
        out_specs=(rows, rows),
        check_vma=False,
    )
```

```python
import functools
import math

import jax
import jax.numpy as jnp
from jax import lax
from jax.experimental import pallas as pl
from jax.experimental.pallas import tpu as pltpu
from jax.sharding import Mesh, PartitionSpec as P

HEADS = 4
DH = 128
NY = 4
NZ = 8
ROWS = 256
CROWS = 32
QROWS = ROWS + CROWS
FOLD = QROWS // 2
REST = ROWS - FOLD
BLOCK = 128
KEYS = NY * ROWS
TOTAL = KEYS + NY * CROWS
NOBODY = 1 << 30
HALF = 1.0 / (2.0 * math.sqrt(DH))
VMEM_LIMIT = 16 * 1024 * 1024
WIDE_LIMIT = 60 * 1024 * 1024
VMEM = pl.BlockSpec(memory_space=pltpu.VMEM)
SMEM = pl.BlockSpec(memory_space=pltpu.SMEM)
PARAMS = pltpu.CompilerParams(vmem_limit_bytes=VMEM_LIMIT)


def contract_lanes(a, b):
    return lax.dot_general(a, b, (((1,), (1,)), ((), ())), preferred_element_type=jnp.float32)


def silu_weight(scores):
    half = scores * HALF
    return (half * jnp.tanh(half) + half).astype(jnp.bfloat16)


def split_kernel(y_ref, k_ref, v_ref, q_ref, c_ref, *outs):
    for i in range(HEADS):
        at = pl.ds(pl.multiple_of(lax.rem(y_ref[0] + i, HEADS) * DH, DH), DH)
        kv, q = outs[i], outs[HEADS + i]
        kv[:, 0:DH] = k_ref[:, at]
        kv[:, DH : 2 * DH] = v_ref[:, at]
        q[:, 0:DH] = q_ref[0:FOLD, at]
        q[0:REST, DH : 2 * DH] = q_ref[FOLD:ROWS, at]
        q[REST:FOLD, DH : 2 * DH] = c_ref[:, at]


def join_kernel(y_ref, *refs):
    *pieces, low, high, whole = refs
    for i, piece in enumerate(pieces):
        strip = lax.rem(y_ref[0] + NY - i, NY)
        whole[pl.ds(pl.multiple_of(strip * ROWS, ROWS), ROWS), :] = piece[...]
    low[...] = whole[0 : 2 * ROWS, :]
    high[...] = whole[2 * ROWS : KEYS, :]


def unfold_kernel(y_ref, *refs):
    *pieces, out = refs
    for i, piece in enumerate(pieces):
        strip = lax.rem(y_ref[0] + NY - i, NY)
        row = pl.multiple_of(strip * ROWS, ROWS)
        out[pl.ds(row, FOLD), :] = piece[:, 0:DH]
        out[pl.ds(pl.multiple_of(row + FOLD, 16), REST), :] = piece[0:REST, DH : 2 * DH]
        out[pl.ds(pl.multiple_of(KEYS + strip * CROWS, CROWS), CROWS), :] = piece[REST:FOLD, DH : 2 * DH]


def attend_kernel(offsets, strips, first, last, z_ref, start_ref, len_ref, qs, user_ref, *refs):
    *kv_refs, in_ref = refs[: len(refs) - (2 if last else 3)] if not first else (*refs[:-3], None)
    out_ref, acc = (refs[-2], refs[-1]) if last else (refs[-3], refs[-1])
    z = z_ref[0]
    starts = [start_ref[u] for u in range(2)]
    ends = [start_ref[u] + len_ref[u] for u in range(2)]
    span = len(strips) * ROWS

    if last:
        (kv,) = kv_refs
    else:
        kv = refs[-2]
        size = kv_refs[0].shape[0]
        for i, ref in enumerate(kv_refs):
            kv[i * size : (i + 1) * size, :] = ref[...]
    if first:
        acc[...] = jnp.zeros_like(acc)
    else:
        acc[...] = in_ref[...]

    lows, stops = [], []
    for half in range(2 * NY):
        event = (half // 2 * NZ + z) * ROWS + half % 2 * BLOCK
        low, stop = jnp.int32(NOBODY), jnp.int32(0)
        for s, t in zip(starts, ends):
            inside = (s <= event) & (event < t)
            low = jnp.where(inside, s, low)
            stop = jnp.where(inside, t, stop)
        lows.append(low)
        stops.append(stop)
    user = user_ref[...]
    cand_low = jnp.where(user == 0, starts[0], starts[1])
    cand_stop = jnp.where(user == 0, ends[0], ends[1])
    column = lax.broadcasted_iota(jnp.int32, (1, ROWS), 1)

    def block_step(block, base, shift):
        for i, strip in enumerate(strips):
            slot = strip + shift
            row = slot * ROWS
            key = pl.multiple_of(base + i * ROWS, ROWS)
            events = (strip * NZ + block) * ROWS + column
            w = silu_weight(contract_lanes(qs[row:TOTAL, :], kv[pl.ds(key, ROWS), 0:DH]))
            parts = []
            for half in range(2 * slot, 2 * NY):
                at = half * BLOCK - row
                keep = jnp.where(events >= lows[half], 1.0, 0.0).astype(jnp.bfloat16)
                parts.append(w[at : at + BLOCK] * keep)
            keep = jnp.where((events >= cand_low) & (events < cand_stop), 1.0, 0.0).astype(jnp.bfloat16)
            parts.append(w[KEYS - row :] * keep)
            w = parts[0] if len(parts) == 1 else jnp.concatenate(parts, axis=0)
            acc[row:TOTAL, :] += jnp.dot(w, kv[pl.ds(key, ROWS), DH : 2 * DH], preferred_element_type=jnp.float32)

    def step(part, carry):
        block = z + offsets[-1]
        for n, offset in enumerate(offsets[:-1]):
            block = jnp.where(part == n, z + offset, block)
        block = lax.rem(block, NZ)
        base = (block if last else part) * span

        @pl.when(block < z)
        def _():
            block_step(block, base, 0)

        @pl.when(block >= z)
        def _():
            block_step(block, base, 1)

        return carry

    lax.fori_loop(0, len(offsets), step, 0)

    if first:
        at = lax.broadcasted_iota(jnp.int32, (BLOCK, ROWS), 0)
        to = lax.broadcasted_iota(jnp.int32, (BLOCK, ROWS), 1)
        for s in range(NY):
            rows = slice(s * ROWS, (s + 1) * ROWS)
            w = silu_weight(contract_lanes(qs[rows, :], kv[rows, 0:DH]))
            event = (s * NZ + z) * ROWS
            parts = []
            for half in range(2):
                mask = (to <= at + half * BLOCK) & (event + to >= lows[2 * s + half])
                parts.append(w[half * BLOCK : (half + 1) * BLOCK] * jnp.where(mask, 1.0, 0.0).astype(jnp.bfloat16))
            w = jnp.concatenate(parts, axis=0)
            acc[rows, :] += jnp.dot(w, kv[rows, DH : 2 * DH], preferred_element_type=jnp.float32)

    if not last:
        out_ref[...] = acc[...]
    else:
        for s in range(NY):
            event = (s * NZ + z) * ROWS
            at = lax.broadcasted_iota(jnp.int32, (ROWS, DH), 0)
            stop = jnp.where(at < BLOCK, stops[2 * s], stops[2 * s + 1])
            rows = jnp.where(event + at < stop, acc[s * ROWS : (s + 1) * ROWS, :], 0.0).astype(jnp.bfloat16)
            out_ref[s * FOLD : (s + 1) * FOLD, 0:DH] = rows[0:FOLD]
            out_ref[s * FOLD : s * FOLD + REST, DH : 2 * DH] = rows[FOLD:ROWS]
            cands = acc[KEYS + s * CROWS : KEYS + (s + 1) * CROWS, :].astype(jnp.bfloat16)
            out_ref[s * FOLD + REST : (s + 1) * FOLD, DH : 2 * DH] = cands


def attend(offsets, strips, where, queries, users, blocks, total, last=False):
    first = total is None
    shape = jax.ShapeDtypeStruct((NY * FOLD, 2 * DH), jnp.bfloat16) if last else jax.ShapeDtypeStruct((TOTAL, DH), jnp.float32)
    state = [] if first else [total]
    keys = len(offsets) * len(strips) * ROWS
    return pl.pallas_call(
        functools.partial(attend_kernel, offsets, strips, first, last),
        in_specs=[SMEM] * 3 + [VMEM] * (2 + len(blocks) + len(state)),
        out_specs=VMEM,
        out_shape=shape,
        scratch_shapes=([] if last else [pltpu.VMEM((keys, 2 * DH), jnp.bfloat16)]) + [pltpu.VMEM((TOTAL, DH), jnp.float32)],
        compiler_params=PARAMS,
        cost_estimate=pl.CostEstimate(flops=4 * TOTAL * keys * DH, bytes_accessed=1 << 20, transcendentals=0),
        name="attend",
    )(*where, queries, users, *blocks, *state)


def finish_kernel(t_ref, hg, hx, cq, ck, cv, cg, cx, w_ref, ho, co):
    hist, cand = [], []
    for h in range(HEADS):
        at = slice(h * DH, (h + 1) * DH)
        rows = t_ref[h * FOLD : (h + 1) * FOLD, :].astype(jnp.float32)
        hist.append(jnp.concatenate([rows[:, 0:DH], rows[0:REST, DH : 2 * DH]], axis=0))
        scores = jnp.sum(cq[:, at].astype(jnp.float32) * ck[:, at].astype(jnp.float32), axis=-1, keepdims=True)
        weight = silu_weight(scores).astype(jnp.float32)
        cand.append(rows[REST:FOLD, DH : 2 * DH] + weight * cv[:, at].astype(jnp.float32))

    def tail(total, gate, inputs, out):
        mean = jnp.mean(total, axis=-1, keepdims=True)
        centered = total - mean
        spread = jnp.mean(centered * centered, axis=-1, keepdims=True)
        normed = centered * lax.rsqrt(spread + 1e-05)
        gated = (normed * gate[...].astype(jnp.float32)).astype(jnp.bfloat16)
        mixed = jnp.dot(gated, w_ref[...], preferred_element_type=jnp.float32)
        out[...] = (inputs[...].astype(jnp.float32) + mixed).astype(jnp.bfloat16)

    tail(jnp.concatenate(hist, axis=1), hg, hx, ho)
    tail(jnp.concatenate(cand, axis=1), cg, cx, co)


def call(kernel, shapes, *args, place=None, scratch=(), limit=VMEM_LIMIT):
    args = args if place is None else (place, *args)
    return pl.pallas_call(
        kernel,
        in_specs=[SMEM] * (place is not None) + [VMEM] * (len(args) - (place is not None)),
        out_specs=[VMEM] * len(shapes),
        out_shape=[jax.ShapeDtypeStruct(s, jnp.bfloat16) for s in shapes],
        scratch_shapes=scratch,
        compiler_params=pltpu.CompilerParams(vmem_limit_bytes=limit),
    )(*args)


def turn(array, axis, step):
    count = NY if axis == "y" else NZ
    return lax.ppermute(array, axis, [(i, (i + step) % count) for i in range(count)])


def on_device(
    hist_query, hist_key, hist_value, hist_gate, hist_input,
    cand_query, cand_key, cand_value, cand_gate, cand_input,
    cand_user, hist_len, hist_start, out_weight,
):
    z = lax.axis_index("z")
    y = lax.axis_index("y").astype(jnp.int32).reshape(1)
    where = (z.astype(jnp.int32).reshape(1), hist_start, hist_len)
    users = lax.dynamic_index_in_dim(cand_user.reshape(NY, NZ, CROWS), z, axis=1).reshape(NY * CROWS, 1)
    parts = call(
        split_kernel, [(ROWS, 2 * DH)] * HEADS + [(FOLD, 2 * DH)] * HEADS,
        hist_key, hist_value, hist_query, cand_query, place=y, limit=WIDE_LIMIT,
    )
    pieces = [parts[0]] + [turn(parts[i], "y", i) for i in (1, 2, 3)]
    folds = [parts[HEADS]] + [turn(parts[HEADS + i], "y", i) for i in (1, 2, 3)]
    near, far = call(
        join_kernel, [(2 * ROWS, 2 * DH)] * 2, *pieces, place=y, scratch=[pltpu.VMEM((KEYS, 2 * DH), jnp.bfloat16)]
    )
    gathered = lax.all_gather(far, "z", axis=0, tiled=True)
    up, down = turn(near, "z", 1), turn(near, "z", -1)
    (queries,) = call(unfold_kernel, [(TOTAL, DH)], *folds, place=y)
    total = attend((0,), (0, 1, 2, 3), where, queries, users, (near, far), None)
    for step in (1, 2):
        up, held = lax.optimization_barrier((up, total))
        down, total = lax.optimization_barrier((down, held))
        blocks = (up, down)
        up, down = turn(up, "z", 1), turn(down, "z", -1)
        total = attend((NZ - step, step), (0, 1), where, queries, users, blocks, total)
    up, held = lax.optimization_barrier((up, total))
    down, total = lax.optimization_barrier((down, held))
    low, high = turn(up[:ROWS], "z", 1), turn(down[ROWS:], "z", -1)
    total = attend((NZ - 3, 3), (0, 1), where, queries, users, (up, down), total)
    total = attend((4,), (0, 1), where, queries, users, (low, high), total)
    total = attend(tuple(range(1, NZ)), (2, 3), where, queries, users, (gathered,), total, last=True)
    total = lax.all_to_all(total, "y", 0, 0, tiled=True)
    return tuple(
        call(
            finish_kernel, [hist_input.shape, cand_input.shape],
            total, hist_gate, hist_input, cand_query, cand_key, cand_value, cand_gate, cand_input, out_weight,
        )
    )


def solution(mesh):
    grid = Mesh(mesh.devices.reshape(-1, NY, NZ), ("batch", "y", "z"))
    rows = P(("batch", "y", "z"), None)
    return jax.shard_map(
        on_device,
        mesh=grid,
        in_specs=(rows,) * 10 + (P("batch"), P("batch"), P("batch"), P()),
        out_specs=(rows, rows),
        check_vma=False,
    )
```

```python
import functools
import math

import jax
import jax.numpy as jnp
from jax import lax
from jax.experimental import pallas as pl
from jax.experimental.pallas import tpu as pltpu
from jax.sharding import Mesh, PartitionSpec as P

HEADS = 4
DH = 128
HD = HEADS * DH
NY = 4
NZ = 8
ROWS = 256
CROWS = 32
QROWS = ROWS + CROWS
BLOCK = 128
HISTS = NY * ROWS
TOTAL = HISTS + NY * CROWS
NOBODY = 1 << 30
HALF = 1.0 / (2.0 * math.sqrt(DH))
VMEM_LIMIT = 20 * 1024 * 1024
WIDE_LIMIT = 60 * 1024 * 1024
VMEM = pl.BlockSpec(memory_space=pltpu.VMEM)
SMEM = pl.BlockSpec(memory_space=pltpu.SMEM)


def contract_lanes(a, b):
    return lax.dot_general(a, b, (((1,), (1,)), ((), ())), preferred_element_type=jnp.float32)


def silu_weight(scores):
    half = scores * HALF
    return (half * jnp.tanh(half) + half).astype(jnp.bfloat16)


def flag(mask):
    return jnp.where(mask, 1.0, 0.0).astype(jnp.bfloat16)


def head(h):
    return slice(h * DH, (h + 1) * DH)


def stack_kernel(k_ref, v_ref, q_ref, c_ref, kv, qc):
    kv[0:ROWS, :] = k_ref[...]
    kv[ROWS : 2 * ROWS, :] = v_ref[...]
    qc[0:ROWS, :] = q_ref[...]
    qc[ROWS:QROWS, :] = c_ref[...]


def attend_kernel(offsets, first, last, place_ref, start_ref, len_ref, user_ref, *refs):
    refs = list(refs)
    if last:
        k_refs, v_refs, kv_row = [refs.pop(0)], [refs.pop(0)], 0
    else:
        k_refs = v_refs = [refs.pop(0) for _ in offsets]
        kv_row = ROWS
    if first:
        pieces = [refs.pop(0) for _ in range(NY)]
        acc, qs = refs
    else:
        qs, in_ref = refs.pop(0), refs.pop(0)
        if last:
            own, *away, acc = refs
        else:
            (acc,) = refs
    y = place_ref[0]
    z = place_ref[1]
    starts = [start_ref[u] for u in range(2)]
    ends = [start_ref[u] + len_ref[u] for u in range(2)]

    if first:
        for slot, piece in enumerate(pieces):
            qs[slot * ROWS : (slot + 1) * ROWS, :] = piece[0:ROWS, :]
            qs[HISTS + slot * CROWS : HISTS + (slot + 1) * CROWS, :] = piece[ROWS:QROWS, :]
        acc[...] = jnp.zeros_like(acc)
    else:
        acc[...] = in_ref[...]

    def owner_of(event):
        low, stop = jnp.int32(NOBODY), jnp.int32(0)
        for s, t in zip(starts, ends):
            inside = (s <= event) & (event < t)
            low = jnp.where(inside, s, low)
            stop = jnp.where(inside, t, stop)
        return low, stop

    column = lax.broadcasted_iota(jnp.int32, (1, ROWS), 1)
    blocks = [lax.rem(z + offset, NZ) for offset in offsets]
    events = [(y * NZ + block) * ROWS + column for block in blocks]

    def weights(rows, i, h):
        return silu_weight(contract_lanes(rows, k_refs[i][0:ROWS, head(h)]))

    def values(i, h):
        return v_refs[i][kv_row : kv_row + ROWS, head(h)]

    def slot_step(slot, carry):
        event = ((y + slot) * NZ + z) * ROWS
        row = pl.multiple_of(slot * ROWS, ROWS)
        low0, _ = owner_of(event)
        low1, _ = owner_of(event + BLOCK)
        keeps = []
        for block, keys in zip(blocks, events):
            late = jnp.where((slot == 0) & (block >= z), NOBODY, 0)
            keeps.append([flag(keys >= jnp.maximum(low, late)) for low in (low0, low1)])
        for h in range(HEADS):
            out = None
            for i in range(len(blocks)):
                w = weights(qs[pl.ds(row, ROWS), head(h)], i, h)
                w = jnp.concatenate([w[0:BLOCK] * keeps[i][0], w[BLOCK:ROWS] * keeps[i][1]], axis=0)
                term = jnp.dot(w, values(i, h), preferred_element_type=jnp.float32)
                out = term if out is None else out + term
            acc[pl.ds(row, ROWS), head(h)] += out
        return carry

    lax.fori_loop(0, NY - y, slot_step, 0)

    user = user_ref[...]
    cand_low = jnp.where(user == 0, starts[0], starts[1])
    cand_stop = jnp.where(user == 0, ends[0], ends[1])
    keeps = [flag((keys >= cand_low) & (keys < cand_stop)) for keys in events]
    for h in range(HEADS):
        out = None
        for i in range(len(blocks)):
            w = weights(qs[HISTS:TOTAL, head(h)], i, h) * keeps[i]
            term = jnp.dot(w, values(i, h), preferred_element_type=jnp.float32)
            out = term if out is None else out + term
        acc[HISTS:TOTAL, head(h)] += out

    if first:
        at = lax.broadcasted_iota(jnp.int32, (ROWS, ROWS), 0)
        to = lax.broadcasted_iota(jnp.int32, (ROWS, ROWS), 1)
        event = (y * NZ + z) * ROWS
        low0, _ = owner_of(event)
        low1, _ = owner_of(event + BLOCK)
        keep = flag((to <= at) & (event + to >= jnp.where(at < BLOCK, low0, low1)))
        for h in range(HEADS):
            w = weights(qs[0:ROWS, head(h)], 0, h) * keep
            acc[0:ROWS, head(h)] += jnp.dot(w, values(0, h), preferred_element_type=jnp.float32)

    if last:
        at = lax.broadcasted_iota(jnp.int32, (ROWS, HD), 0)
        for slot in range(NY):
            event = ((y + slot) * NZ + z) * ROWS
            _, stop0 = owner_of(event)
            _, stop1 = owner_of(event + BLOCK)
            stop = jnp.where(at < BLOCK, stop0, stop1)
            out = own if slot == 0 else away[slot - 1]
            rows = jnp.where(event + at < stop, acc[slot * ROWS : (slot + 1) * ROWS, :], 0.0)
            out[0:ROWS, :] = rows.astype(out.dtype)
            out[ROWS:QROWS, :] = acc[HISTS + slot * CROWS : HISTS + (slot + 1) * CROWS, :].astype(out.dtype)


def attend(offsets, where, users, blocks, queries, total, last=False):
    first = total is None
    state = jax.ShapeDtypeStruct((TOTAL, HD), jnp.float32)
    if last:
        shapes = [jax.ShapeDtypeStruct((QROWS, HD), jnp.float32)] + [jax.ShapeDtypeStruct((QROWS, HD), jnp.bfloat16)] * 3
    elif first:
        shapes = [state, jax.ShapeDtypeStruct((TOTAL, HD), jnp.bfloat16)]
    else:
        shapes = [state]
    args = [*blocks, *queries] if first else [*blocks, queries, total]
    return pl.pallas_call(
        functools.partial(attend_kernel, offsets, first, last),
        in_specs=[SMEM] * 3 + [VMEM] * (1 + len(args)),
        out_specs=[VMEM] * len(shapes),
        out_shape=shapes,
        scratch_shapes=[pltpu.VMEM((TOTAL, HD), jnp.float32)] * last,
        compiler_params=pltpu.CompilerParams(vmem_limit_bytes=VMEM_LIMIT),
        cost_estimate=pl.CostEstimate(
            flops=4 * TOTAL * len(offsets) * ROWS * HD, bytes_accessed=1 << 20, transcendentals=0
        ),
        name="attend",
    )(*where, users, *args)


def finish_kernel(t0, t1, t2, t3, hg, hx, cq, ck, cv, cg, cx, w_ref, ho, co):
    total = t0[...]
    for part in (t1, t2, t3):
        total = total + part[...].astype(jnp.float32)
    own = []
    for h in range(HEADS):
        scores = jnp.sum(cq[:, head(h)].astype(jnp.float32) * ck[:, head(h)].astype(jnp.float32), axis=-1, keepdims=True)
        own.append(silu_weight(scores).astype(jnp.float32) * cv[:, head(h)].astype(jnp.float32))

    def tail(rows, gate, inputs, out):
        mean = jnp.mean(rows, axis=-1, keepdims=True)
        centered = rows - mean
        spread = jnp.mean(centered * centered, axis=-1, keepdims=True)
        normed = centered * lax.rsqrt(spread + 1e-05)
        gated = (normed * gate[...].astype(jnp.float32)).astype(jnp.bfloat16)
        mixed = jnp.dot(gated, w_ref[...], preferred_element_type=jnp.float32)
        out[...] = (inputs[...].astype(jnp.float32) + mixed).astype(jnp.bfloat16)

    tail(total[0:ROWS], hg, hx, ho)
    tail(total[ROWS:QROWS] + jnp.concatenate(own, axis=1), cg, cx, co)


def call(kernel, shapes, *args, limit=VMEM_LIMIT):
    return pl.pallas_call(
        kernel,
        in_specs=[VMEM] * len(args),
        out_specs=[VMEM] * len(shapes),
        out_shape=[jax.ShapeDtypeStruct(s, jnp.bfloat16) for s in shapes],
        compiler_params=pltpu.CompilerParams(vmem_limit_bytes=limit),
    )(*args)


def turn(array, axis, step):
    count = NY if axis == "y" else NZ
    return lax.ppermute(array, axis, [(i, (i + step) % count) for i in range(count)])


def on_device(
    hist_query, hist_key, hist_value, hist_gate, hist_input,
    cand_query, cand_key, cand_value, cand_gate, cand_input,
    cand_user, hist_len, hist_start, out_weight,
):
    y, z = lax.axis_index("y"), lax.axis_index("z")
    where = (jnp.stack([y, z]).astype(jnp.int32), hist_start, hist_len)
    users = lax.dynamic_index_in_dim(cand_user.reshape(NY, NZ, CROWS), z, axis=1, keepdims=False)
    users = lax.dynamic_slice_in_dim(jnp.concatenate([users, users]), y, NY).reshape(NY * CROWS, 1)
    kv, mine = call(
        stack_kernel, [(2 * ROWS, HD), (QROWS, HD)], hist_key, hist_value, hist_query, cand_query, limit=WIDE_LIMIT
    )
    up, down = turn(kv, "z", 1), turn(kv, "z", -1)
    queries = [mine] + [turn(mine, "y", -k) for k in (1, 2, 3)]
    up, *queries = lax.optimization_barrier((up, *queries))
    blocks = (kv, up, down)
    up, down = turn(up, "z", 1), turn(down, "z", -1)
    total, queries = attend((0, NZ - 1, 1), where, users, blocks, queries, None)
    up, held = lax.optimization_barrier((up, total))
    down, total = lax.optimization_barrier((down, held))
    blocks = (up, down)
    up, down = turn(up, "z", 1), turn(down, "z", -1)
    (total,) = attend((NZ - 2, 2), where, users, blocks, queries, total)
    up, held = lax.optimization_barrier((up, total))
    down, total = lax.optimization_barrier((down, held))
    keys, values = turn(up[:ROWS], "z", 1), turn(down[ROWS:], "z", -1)
    (total,) = attend((NZ - 3, 3), where, users, (up, down), queries, total)
    own, *away = attend((4,), where, users, (keys, values), queries, total, last=True)
    back = [turn(a, "y", k) for k, a in zip((1, 2, 3), away)]
    return tuple(
        call(
            finish_kernel, [hist_input.shape, cand_input.shape],
            own, *back, hist_gate, hist_input, cand_query, cand_key, cand_value, cand_gate, cand_input, out_weight,
        )
    )


def solution(mesh):
    grid = Mesh(mesh.devices.reshape(-1, NY, NZ), ("batch", "y", "z"))
    rows = P(("batch", "y", "z"), None)
    return jax.shard_map(
        on_device,
        mesh=grid,
        in_specs=(rows,) * 10 + (P("batch"), P("batch"), P("batch"), P()),
        out_specs=(rows, rows),
        check_vma=False,
    )
```

```python
import functools
import math

import jax
import jax.numpy as jnp
from jax import lax
from jax.experimental import pallas as pl
from jax.experimental.pallas import tpu as pltpu
from jax.sharding import Mesh, PartitionSpec as P

HEADS = 4
DH = 128
HD = HEADS * DH
NY = 4
NZ = 8
ROWS = 256
CROWS = 32
QROWS = ROWS + CROWS
BLOCK = 128
HISTS = NY * ROWS
TOTAL = HISTS + NY * CROWS
NOBODY = 1 << 30
HALF = 1.0 / (2.0 * math.sqrt(DH))
VMEM_LIMIT = 20 * 1024 * 1024
WIDE_LIMIT = 60 * 1024 * 1024
VMEM = pl.BlockSpec(memory_space=pltpu.VMEM)
SMEM = pl.BlockSpec(memory_space=pltpu.SMEM)


def contract_lanes(a, b):
    return lax.dot_general(a, b, (((1,), (1,)), ((), ())), preferred_element_type=jnp.float32)


def silu_weight(scores):
    half = scores * HALF
    return (half * jnp.tanh(half) + half).astype(jnp.bfloat16)


def flag(mask):
    return jnp.where(mask, 1.0, 0.0).astype(jnp.bfloat16)


def head(h):
    return slice(h * DH, (h + 1) * DH)


def stack_kernel(k_ref, v_ref, q_ref, c_ref, kv, qc):
    kv[0:ROWS, :] = k_ref[...]
    kv[ROWS : 2 * ROWS, :] = v_ref[...]
    qc[0:ROWS, :] = q_ref[...]
    qc[ROWS:QROWS, :] = c_ref[...]


def attend_kernel(offsets, first, last, place_ref, start_ref, len_ref, user_ref, *refs):
    refs = list(refs)
    blocks = [refs.pop(0) for _ in offsets]
    if first:
        pieces = [refs.pop(0) for _ in range(NY)]
        acc, qs, kv = refs
    else:
        qs, in_ref = refs.pop(0), refs.pop(0)
        if last:
            own, *away, acc, kv = refs
        else:
            acc, kv = refs
    y = place_ref[0]
    z = place_ref[1]
    starts = [start_ref[u] for u in range(2)]
    ends = [start_ref[u] + len_ref[u] for u in range(2)]

    for i, block in enumerate(blocks):
        kv[i * 2 * ROWS : (i + 1) * 2 * ROWS, :] = block[...]
    if first:
        for slot, piece in enumerate(pieces):
            at = (NY - 1 - slot) * ROWS
            qs[at : at + ROWS, :] = piece[0:ROWS, :]
            qs[HISTS + slot * CROWS : HISTS + (slot + 1) * CROWS, :] = piece[ROWS:QROWS, :]
        acc[...] = jnp.zeros_like(acc)
    else:
        acc[...] = in_ref[...]

    lows, stops = [], []
    for half in range(2 * NY):
        event = ((y + NY - 1 - half // 2) * NZ + z) * ROWS + half % 2 * BLOCK
        low, stop = jnp.int32(NOBODY), jnp.int32(0)
        for s, t in zip(starts, ends):
            inside = (s <= event) & (event < t)
            low = jnp.where(inside, s, low)
            stop = jnp.where(inside, t, stop)
        lows.append(low)
        stops.append(stop)
    user = user_ref[...]
    cand_low = jnp.where(user == 0, starts[0], starts[1])
    cand_stop = jnp.where(user == 0, ends[0], ends[1])
    column = lax.broadcasted_iota(jnp.int32, (1, ROWS), 1)

    def block_step(skip, part):
        block = z + offsets[-1]
        for n, offset in enumerate(offsets[:-1]):
            block = jnp.where(part == n, z + offset, block)
        block = lax.rem(block, NZ)
        late = jnp.where(block >= z, NOBODY, 0)
        events = (y * NZ + block) * ROWS + column
        keeps = []
        for half in range(2 * skip, 2 * NY):
            low = lows[half] if half < 2 * NY - 2 else jnp.maximum(lows[half], late)
            keeps.append(flag(events >= low))
        keeps.append(flag((events >= cand_low) & (events < cand_stop)))
        key = pl.multiple_of(part * 2 * ROWS, ROWS)
        for h in range(HEADS):
            w = silu_weight(contract_lanes(qs[skip * ROWS : TOTAL, head(h)], kv[pl.ds(key, ROWS), head(h)]))
            w = jnp.concatenate([w[i * BLOCK : (i + 1) * BLOCK] * keep for i, keep in enumerate(keeps)], axis=0)
            v = kv[pl.ds(pl.multiple_of(key + ROWS, ROWS), ROWS), head(h)]
            acc[skip * ROWS : TOTAL, head(h)] += jnp.dot(w, v, preferred_element_type=jnp.float32)

    for skip in range(NY):

        @pl.when(y == skip)
        def _(skip=skip):
            def step(part, carry):
                block_step(skip, part)
                return carry

            lax.fori_loop(0, len(offsets), step, 0)

    if first:
        at = lax.broadcasted_iota(jnp.int32, (ROWS, ROWS), 0)
        to = lax.broadcasted_iota(jnp.int32, (ROWS, ROWS), 1)
        event = (y * NZ + z) * ROWS
        keep = flag((to <= at) & (event + to >= jnp.where(at < BLOCK, lows[-2], lows[-1])))
        rows = slice(HISTS - ROWS, HISTS)
        for h in range(HEADS):
            w = silu_weight(contract_lanes(qs[rows, head(h)], kv[0:ROWS, head(h)])) * keep
            acc[rows, head(h)] += jnp.dot(w, kv[ROWS : 2 * ROWS, head(h)], preferred_element_type=jnp.float32)

    if last:
        at = lax.broadcasted_iota(jnp.int32, (ROWS, HD), 0)
        for slot in range(NY):
            event = ((y + slot) * NZ + z) * ROWS
            row = (NY - 1 - slot) * ROWS
            half = 2 * (NY - 1 - slot)
            stop = jnp.where(at < BLOCK, stops[half], stops[half + 1])
            out = own if slot == 0 else away[slot - 1]
            out[0:ROWS, :] = jnp.where(event + at < stop, acc[row : row + ROWS, :], 0.0).astype(out.dtype)
            out[ROWS:QROWS, :] = acc[HISTS + slot * CROWS : HISTS + (slot + 1) * CROWS, :].astype(out.dtype)


def attend(offsets, where, users, blocks, queries, total, last=False):
    first = total is None
    state = jax.ShapeDtypeStruct((TOTAL, HD), jnp.float32)
    if last:
        shapes = [jax.ShapeDtypeStruct((QROWS, HD), jnp.float32)] + [jax.ShapeDtypeStruct((QROWS, HD), jnp.bfloat16)] * 3
    elif first:
        shapes = [state, jax.ShapeDtypeStruct((TOTAL, HD), jnp.bfloat16)]
    else:
        shapes = [state]
    args = [*blocks, *queries] if first else [*blocks, queries, total]
    return pl.pallas_call(
        functools.partial(attend_kernel, offsets, first, last),
        in_specs=[SMEM] * 3 + [VMEM] * (1 + len(args)),
        out_specs=[VMEM] * len(shapes),
        out_shape=shapes,
        scratch_shapes=[pltpu.VMEM((TOTAL, HD), jnp.float32)] * last
        + [pltpu.VMEM((len(offsets) * 2 * ROWS, HD), jnp.bfloat16)],
        compiler_params=pltpu.CompilerParams(vmem_limit_bytes=VMEM_LIMIT),
        cost_estimate=pl.CostEstimate(
            flops=4 * TOTAL * len(offsets) * ROWS * HD, bytes_accessed=1 << 20, transcendentals=0
        ),
        name="attend",
    )(*where, users, *args)


def finish_kernel(t0, t1, t2, t3, hg, hx, cq, ck, cv, cg, cx, w_ref, ho, co):
    total = t0[...]
    for part in (t1, t2, t3):
        total = total + part[...].astype(jnp.float32)
    own = []
    for h in range(HEADS):
        scores = jnp.sum(cq[:, head(h)].astype(jnp.float32) * ck[:, head(h)].astype(jnp.float32), axis=-1, keepdims=True)
        own.append(silu_weight(scores).astype(jnp.float32) * cv[:, head(h)].astype(jnp.float32))

    def tail(rows, gate, inputs, out):
        mean = jnp.mean(rows, axis=-1, keepdims=True)
        centered = rows - mean
        spread = jnp.mean(centered * centered, axis=-1, keepdims=True)
        normed = centered * lax.rsqrt(spread + 1e-05)
        gated = (normed * gate[...].astype(jnp.float32)).astype(jnp.bfloat16)
        mixed = jnp.dot(gated, w_ref[...], preferred_element_type=jnp.float32)
        out[...] = (inputs[...].astype(jnp.float32) + mixed).astype(jnp.bfloat16)

    tail(total[0:ROWS], hg, hx, ho)
    tail(total[ROWS:QROWS] + jnp.concatenate(own, axis=1), cg, cx, co)


def call(kernel, shapes, *args, limit=VMEM_LIMIT):
    return pl.pallas_call(
        kernel,
        in_specs=[VMEM] * len(args),
        out_specs=[VMEM] * len(shapes),
        out_shape=[jax.ShapeDtypeStruct(s, jnp.bfloat16) for s in shapes],
        compiler_params=pltpu.CompilerParams(vmem_limit_bytes=limit),
    )(*args)


def turn(array, axis, step):
    count = NY if axis == "y" else NZ
    return lax.ppermute(array, axis, [(i, (i + step) % count) for i in range(count)])


def on_device(
    hist_query, hist_key, hist_value, hist_gate, hist_input,
    cand_query, cand_key, cand_value, cand_gate, cand_input,
    cand_user, hist_len, hist_start, out_weight,
):
    y, z = lax.axis_index("y"), lax.axis_index("z")
    where = (jnp.stack([y, z]).astype(jnp.int32), hist_start, hist_len)
    users = lax.dynamic_index_in_dim(cand_user.reshape(NY, NZ, CROWS), z, axis=1, keepdims=False)
    users = lax.dynamic_slice_in_dim(jnp.concatenate([users, users]), y, NY).reshape(NY * CROWS, 1)
    kv, mine = call(
        stack_kernel, [(2 * ROWS, HD), (QROWS, HD)], hist_key, hist_value, hist_query, cand_query, limit=WIDE_LIMIT
    )
    blocks, queries = [(kv, kv)], [mine]
    for step in range(3):
        up, down = blocks[-1]
        if step:
            up, _ = lax.optimization_barrier((up, queries[-1]))
            down, _ = lax.optimization_barrier((down, queries[-1]))
        blocks.append((turn(up, "z", 1), turn(down, "z", -1)))
        queries.append(turn(queries[-1], "y", -1))
    across = turn(blocks[3][0], "z", 1)
    total, stacked = attend((0, NZ - 1, 1), where, users, (kv, *blocks[1]), queries, None)
    for step in (2, 3):
        (total,) = attend((NZ - step, step), where, users, blocks[step], stacked, total)
    own, *away = attend((4,), where, users, (across,), stacked, total, last=True)
    back = [turn(a, "y", k) for k, a in zip((1, 2, 3), away)]
    return tuple(
        call(
            finish_kernel, [hist_input.shape, cand_input.shape],
            own, *back, hist_gate, hist_input, cand_query, cand_key, cand_value, cand_gate, cand_input, out_weight,
        )
    )


def solution(mesh):
    grid = Mesh(mesh.devices.reshape(-1, NY, NZ), ("batch", "y", "z"))
    rows = P(("batch", "y", "z"), None)
    return jax.shard_map(
        on_device,
        mesh=grid,
        in_specs=(rows,) * 10 + (P("batch"), P("batch"), P("batch"), P()),
        out_specs=(rows, rows),
        check_vma=False,
    )
```

```python
import functools
import math

import jax
import jax.numpy as jnp
from jax import lax
from jax.experimental import pallas as pl
from jax.experimental.pallas import tpu as pltpu
from jax.sharding import Mesh, PartitionSpec as P

HEADS = 4
DH = 128
NY = 4
NZ = 8
ROWS = 256
CROWS = 32
QROWS = ROWS + CROWS
FOLD = QROWS // 2
REST = ROWS - FOLD
PART = ROWS + FOLD
BLOCK = 128
KEYS = NY * ROWS
TOTAL = KEYS + NY * CROWS
NOBODY = 1 << 30
HALF = 1.0 / (2.0 * math.sqrt(DH))
VMEM_LIMIT = 16 * 1024 * 1024
WIDE_LIMIT = 60 * 1024 * 1024
VMEM = pl.BlockSpec(memory_space=pltpu.VMEM)
SMEM = pl.BlockSpec(memory_space=pltpu.SMEM)
PARAMS = pltpu.CompilerParams(vmem_limit_bytes=VMEM_LIMIT)


def contract_lanes(a, b):
    return lax.dot_general(a, b, (((1,), (1,)), ((), ())), preferred_element_type=jnp.float32)


def silu_weight(scores):
    half = scores * HALF
    return (half * jnp.tanh(half) + half).astype(jnp.bfloat16)


def split_kernel(k_ref, v_ref, q_ref, c_ref, out_ref):
    for h in range(HEADS):
        at = slice(h * DH, (h + 1) * DH)
        row = h * PART
        out_ref[row : row + ROWS, 0:DH] = k_ref[:, at]
        out_ref[row : row + ROWS, DH : 2 * DH] = v_ref[:, at]
        row += ROWS
        out_ref[row : row + FOLD, 0:DH] = q_ref[0:FOLD, at]
        out_ref[row : row + REST, DH : 2 * DH] = q_ref[FOLD:ROWS, at]
        out_ref[row + REST : row + FOLD, DH : 2 * DH] = c_ref[:, at]


def attend_kernel(offsets, first, last, info_ref, q_ref, user_ref, *refs):
    kv_refs = refs[: len(offsets)]
    refs = refs[len(offsets) :]
    if not first:
        in_ref, *refs = refs
    out_ref, kv, qs, acc = refs
    z = info_ref[0]
    starts = [info_ref[1 + u] for u in range(2)]
    ends = [info_ref[1 + u] + info_ref[3 + u] for u in range(2)]

    for i, ref in enumerate(kv_refs):
        kv[i * KEYS : (i + 1) * KEYS, :] = ref[...]
    for s in range(NY):
        row = s * PART + ROWS
        qs[s * ROWS : s * ROWS + FOLD, :] = q_ref[row : row + FOLD, 0:DH]
        qs[s * ROWS + FOLD : (s + 1) * ROWS, :] = q_ref[row : row + REST, DH : 2 * DH]
        qs[KEYS + s * CROWS : KEYS + (s + 1) * CROWS, :] = q_ref[row + REST : row + FOLD, DH : 2 * DH]
    if first:
        acc[...] = jnp.zeros_like(acc)
    else:
        acc[...] = in_ref[...]

    lows, stops = [], []
    for half in range(2 * NY):
        event = (half // 2 * NZ + z) * ROWS + half % 2 * BLOCK
        low, stop = jnp.int32(NOBODY), jnp.int32(0)
        for s, t in zip(starts, ends):
            inside = (s <= event) & (event < t)
            low = jnp.where(inside, s, low)
            stop = jnp.where(inside, t, stop)
        lows.append(low)
        stops.append(stop)
    user = user_ref[...]
    cand_low = jnp.where(user == 0, starts[0], starts[1])
    cand_stop = jnp.where(user == 0, ends[0], ends[1])
    column = lax.broadcasted_iota(jnp.int32, (1, ROWS), 1)

    def block_step(part, slots):
        block = z + offsets[-1]
        for n, offset in enumerate(offsets[:-1]):
            block = jnp.where(part == n, z + offset, block)
        block = lax.rem(block, NZ)
        for strip, slot in enumerate(slots):
            row = slot * ROWS
            key = pl.multiple_of(part * KEYS + strip * ROWS, ROWS)
            events = (strip * NZ + block) * ROWS + column
            w = silu_weight(contract_lanes(qs[row:TOTAL, :], kv[pl.ds(key, ROWS), 0:DH]))
            parts = []
            for half in range(2 * slot, 2 * NY):
                at = half * BLOCK - row
                keep = jnp.where(events >= lows[half], 1.0, 0.0).astype(jnp.bfloat16)
                parts.append(w[at : at + BLOCK] * keep)
            keep = jnp.where((events >= cand_low) & (events < cand_stop), 1.0, 0.0).astype(jnp.bfloat16)
            parts.append(w[KEYS - row :] * keep)
            w = parts[0] if len(parts) == 1 else jnp.concatenate(parts, axis=0)
            acc[row:TOTAL, :] += jnp.dot(w, kv[pl.ds(key, ROWS), DH : 2 * DH], preferred_element_type=jnp.float32)

    def step(part, carry):
        block = z + offsets[-1]
        for n, offset in enumerate(offsets[:-1]):
            block = jnp.where(part == n, z + offset, block)
        before = lax.rem(block, NZ) < z

        @pl.when(before)
        def _():
            block_step(part, range(0, NY))

        @pl.when(jnp.logical_not(before))
        def _():
            block_step(part, range(1, NY + 1))

        return carry

    lax.fori_loop(0, len(offsets), step, 0)

    if first:
        at = lax.broadcasted_iota(jnp.int32, (BLOCK, ROWS), 0)
        to = lax.broadcasted_iota(jnp.int32, (BLOCK, ROWS), 1)
        for s in range(NY):
            rows = slice(s * ROWS, (s + 1) * ROWS)
            w = silu_weight(contract_lanes(qs[rows, :], kv[rows, 0:DH]))
            event = (s * NZ + z) * ROWS
            parts = []
            for half in range(2):
                mask = (to <= at + half * BLOCK) & (event + to >= lows[2 * s + half])
                parts.append(w[half * BLOCK : (half + 1) * BLOCK] * jnp.where(mask, 1.0, 0.0).astype(jnp.bfloat16))
            w = jnp.concatenate(parts, axis=0)
            acc[rows, :] += jnp.dot(w, kv[rows, DH : 2 * DH], preferred_element_type=jnp.float32)

    if not last:
        out_ref[...] = acc[...]
    else:
        for s in range(NY):
            event = (s * NZ + z) * ROWS
            at = lax.broadcasted_iota(jnp.int32, (ROWS, DH), 0)
            stop = jnp.where(at < BLOCK, stops[2 * s], stops[2 * s + 1])
            rows = jnp.where(event + at < stop, acc[s * ROWS : (s + 1) * ROWS, :], 0.0).astype(jnp.bfloat16)
            out_ref[s * FOLD : (s + 1) * FOLD, 0:DH] = rows[0:FOLD]
            out_ref[s * FOLD : s * FOLD + REST, DH : 2 * DH] = rows[FOLD:ROWS]
            cands = acc[KEYS + s * CROWS : KEYS + (s + 1) * CROWS, :].astype(jnp.bfloat16)
            out_ref[s * FOLD + REST : (s + 1) * FOLD, DH : 2 * DH] = cands


def attend(offsets, info, queries, users, blocks, total, last):
    first = total is None
    shape = jax.ShapeDtypeStruct((NY * FOLD, 2 * DH), jnp.bfloat16) if last else jax.ShapeDtypeStruct((TOTAL, DH), jnp.float32)
    state = [] if first else [total]
    return pl.pallas_call(
        functools.partial(attend_kernel, offsets, first, last),
        in_specs=[SMEM] + [VMEM] * (2 + len(blocks) + len(state)),
        out_specs=VMEM,
        out_shape=shape,
        scratch_shapes=[
            pltpu.VMEM((len(offsets) * KEYS, 2 * DH), jnp.bfloat16),
            pltpu.VMEM((TOTAL, DH), jnp.bfloat16),
            pltpu.VMEM((TOTAL, DH), jnp.float32),
        ],
        compiler_params=PARAMS,
        cost_estimate=pl.CostEstimate(
            flops=len(offsets) * 4 * TOTAL * KEYS * DH, bytes_accessed=len(offsets) << 20, transcendentals=0
        ),
        name="attend",
    )(info, queries, users, *blocks, *state)


def finish_kernel(t_ref, hg, hx, cq, ck, cv, cg, cx, w_ref, ho, co):
    hist, cand = [], []
    for h in range(HEADS):
        at = slice(h * DH, (h + 1) * DH)
        rows = t_ref[h * FOLD : (h + 1) * FOLD, :].astype(jnp.float32)
        hist.append(jnp.concatenate([rows[:, 0:DH], rows[0:REST, DH : 2 * DH]], axis=0))
        scores = jnp.sum(cq[:, at].astype(jnp.float32) * ck[:, at].astype(jnp.float32), axis=-1, keepdims=True)
        weight = silu_weight(scores).astype(jnp.float32)
        cand.append(rows[REST:FOLD, DH : 2 * DH] + weight * cv[:, at].astype(jnp.float32))

    def tail(total, gate, inputs, out):
        mean = jnp.mean(total, axis=-1, keepdims=True)
        centered = total - mean
        spread = jnp.mean(centered * centered, axis=-1, keepdims=True)
        normed = centered * lax.rsqrt(spread + 1e-05)
        gated = (normed * gate[...].astype(jnp.float32)).astype(jnp.bfloat16)
        mixed = jnp.dot(gated, w_ref[...], preferred_element_type=jnp.float32)
        out[...] = (inputs[...].astype(jnp.float32) + mixed).astype(jnp.bfloat16)

    tail(jnp.concatenate(hist, axis=1), hg, hx, ho)
    tail(jnp.concatenate(cand, axis=1), cg, cx, co)


def call(kernel, shapes, *args, limit=VMEM_LIMIT):
    return pl.pallas_call(
        kernel,
        in_specs=[VMEM] * len(args),
        out_specs=[VMEM] * len(shapes),
        out_shape=[jax.ShapeDtypeStruct(s, jnp.bfloat16) for s in shapes],
        compiler_params=pltpu.CompilerParams(vmem_limit_bytes=limit),
    )(*args)


def turn(array, step):
    return lax.ppermute(array, "z", [(i, (i + step) % NZ) for i in range(NZ)])


def spread(array):
    return lax.all_to_all(array, "y", 0, 0, tiled=True)


def on_device(
    hist_query, hist_key, hist_value, hist_gate, hist_input,
    cand_query, cand_key, cand_value, cand_gate, cand_input,
    cand_user, hist_len, hist_start, out_weight,
):
    z = lax.axis_index("z")
    info = jnp.concatenate([z.astype(jnp.int32).reshape(1), hist_start, hist_len])
    users = lax.dynamic_index_in_dim(cand_user.reshape(NY, NZ, CROWS), z, axis=1).reshape(NY * CROWS, 1)
    (parts,) = call(
        split_kernel, [(HEADS * PART, 2 * DH)], hist_key, hist_value, hist_query, cand_query, limit=WIDE_LIMIT
    )
    queries = spread(parts)
    own = queries.reshape(NY, PART, 2 * DH)[:, :ROWS].reshape(KEYS, 2 * DH)
    up, down = turn(own, 1), turn(own, -1)
    total = attend((0,), info, queries, users, (own,), None, False)
    for step in (1, 2):
        up, held = lax.optimization_barrier((up, total))
        down, total = lax.optimization_barrier((down, held))
        blocks = (up, down)
        up, down = turn(up, 1), turn(down, -1)
        total = attend((NZ - step, step), info, queries, users, blocks, total, False)
    up, total = lax.optimization_barrier((up, total))
    across = turn(up, 1)
    total = attend((NZ - 3, 3), info, queries, users, (up, down), total, False)
    total = attend((4,), info, queries, users, (across,), total, True)
    return tuple(
        call(
            finish_kernel, [hist_input.shape, cand_input.shape],
            spread(total), hist_gate, hist_input, cand_query, cand_key, cand_value, cand_gate, cand_input, out_weight,
        )
    )


def solution(mesh):
    grid = Mesh(mesh.devices.reshape(-1, NY, NZ), ("batch", "y", "z"))
    rows = P(("batch", "y", "z"), None)
    return jax.shard_map(
        on_device,
        mesh=grid,
        in_specs=(rows,) * 10 + (P("batch"), P("batch"), P("batch"), P()),
        out_specs=(rows, rows),
        check_vma=False,
    )
```

```python
import functools
import math

import jax
import jax.numpy as jnp
from jax import lax
from jax.experimental import pallas as pl
from jax.experimental.pallas import tpu as pltpu
from jax.sharding import Mesh, PartitionSpec as P

HEADS = 4
DH = 128
NY = 4
NZ = 8
ROWS = 256
CROWS = 32
QROWS = ROWS + CROWS
FOLD = QROWS // 2
REST = ROWS - FOLD
BLOCK = 128
KEYS = NY * ROWS
TOTAL = KEYS + NY * CROWS
NOBODY = 1 << 30
HALF = 1.0 / (2.0 * math.sqrt(DH))
VMEM_LIMIT = 16 * 1024 * 1024
WIDE_LIMIT = 60 * 1024 * 1024
VMEM = pl.BlockSpec(memory_space=pltpu.VMEM)
SMEM = pl.BlockSpec(memory_space=pltpu.SMEM)
PARAMS = pltpu.CompilerParams(vmem_limit_bytes=VMEM_LIMIT)


def contract_lanes(a, b):
    return lax.dot_general(a, b, (((1,), (1,)), ((), ())), preferred_element_type=jnp.float32)


def silu_weight(scores):
    half = scores * HALF
    return (half * jnp.tanh(half) + half).astype(jnp.bfloat16)


def split_kernel(y_ref, k_ref, v_ref, q_ref, c_ref, *outs):
    for i in range(HEADS):
        at = pl.ds(pl.multiple_of(lax.rem(y_ref[0] + i, HEADS) * DH, DH), DH)
        kv, q = outs[i], outs[HEADS + i]
        kv[:, 0:DH] = k_ref[:, at]
        kv[:, DH : 2 * DH] = v_ref[:, at]
        q[:, 0:DH] = q_ref[0:FOLD, at]
        q[0:REST, DH : 2 * DH] = q_ref[FOLD:ROWS, at]
        q[REST:FOLD, DH : 2 * DH] = c_ref[:, at]


def join_kernel(y_ref, *refs):
    *pieces, out = refs
    for i, piece in enumerate(pieces):
        strip = lax.rem(y_ref[0] + NY - i, NY)
        out[pl.ds(pl.multiple_of(strip * ROWS, ROWS), ROWS), :] = piece[...]


def unfold_kernel(y_ref, *refs):
    *pieces, out = refs
    for i, piece in enumerate(pieces):
        strip = lax.rem(y_ref[0] + NY - i, NY)
        row = pl.multiple_of(strip * ROWS, ROWS)
        out[pl.ds(row, FOLD), :] = piece[:, 0:DH]
        out[pl.ds(pl.multiple_of(row + FOLD, 16), REST), :] = piece[0:REST, DH : 2 * DH]
        out[pl.ds(pl.multiple_of(KEYS + strip * CROWS, CROWS), CROWS), :] = piece[REST:FOLD, DH : 2 * DH]


def attend_kernel(offsets, first, last, info_ref, qs, user_ref, *refs):
    *ins, out_ref, kv, acc = refs
    z = info_ref[0]
    starts = [info_ref[1 + u] for u in range(2)]
    ends = [info_ref[1 + u] + info_ref[3 + u] for u in range(2)]

    for i in range(len(offsets)):
        kv[i * KEYS : (i + 1) * KEYS, :] = ins[i][...]
    if first:
        acc[...] = jnp.zeros_like(acc)
    else:
        acc[...] = ins[-1][...]

    lows, stops = [], []
    for half in range(2 * NY):
        event = (half // 2 * NZ + z) * ROWS + half % 2 * BLOCK
        low, stop = jnp.int32(NOBODY), jnp.int32(0)
        for s, t in zip(starts, ends):
            inside = (s <= event) & (event < t)
            low = jnp.where(inside, s, low)
            stop = jnp.where(inside, t, stop)
        lows.append(low)
        stops.append(stop)
    user = user_ref[...]
    cand_low = jnp.where(user == 0, starts[0], starts[1])
    cand_stop = jnp.where(user == 0, ends[0], ends[1])
    column = lax.broadcasted_iota(jnp.int32, (1, ROWS), 1)

    def block_step(block, base, shift):
        for strip in range(NY):
            row = (strip + shift) * ROWS
            key = pl.multiple_of(base + strip * ROWS, ROWS)
            events = (strip * NZ + block) * ROWS + column
            w = silu_weight(contract_lanes(qs[row:TOTAL, :], kv[pl.ds(key, ROWS), 0:DH]))
            parts = []
            for half in range(2 * (strip + shift), 2 * NY):
                at = half * BLOCK - row
                keep = jnp.where(events >= lows[half], 1.0, 0.0).astype(jnp.bfloat16)
                parts.append(w[at : at + BLOCK] * keep)
            keep = jnp.where((events >= cand_low) & (events < cand_stop), 1.0, 0.0).astype(jnp.bfloat16)
            parts.append(w[KEYS - row :] * keep)
            w = parts[0] if len(parts) == 1 else jnp.concatenate(parts, axis=0)
            acc[row:TOTAL, :] += jnp.dot(w, kv[pl.ds(key, ROWS), DH : 2 * DH], preferred_element_type=jnp.float32)

    def step(part, carry):
        block = z + offsets[-1]
        for n, offset in enumerate(offsets[:-1]):
            block = jnp.where(part == n, z + offset, block)
        block = lax.rem(block, NZ)

        @pl.when(block < z)
        def _():
            block_step(block, part * KEYS, 0)

        @pl.when(block >= z)
        def _():
            block_step(block, part * KEYS, 1)

        return carry

    lax.fori_loop(0, len(offsets), step, 0)

    if first:
        at = lax.broadcasted_iota(jnp.int32, (BLOCK, ROWS), 0)
        to = lax.broadcasted_iota(jnp.int32, (BLOCK, ROWS), 1)
        for s in range(NY):
            rows = slice(s * ROWS, (s + 1) * ROWS)
            w = silu_weight(contract_lanes(qs[rows, :], kv[rows, 0:DH]))
            event = (s * NZ + z) * ROWS
            parts = []
            for half in range(2):
                mask = (to <= at + half * BLOCK) & (event + to >= lows[2 * s + half])
                parts.append(w[half * BLOCK : (half + 1) * BLOCK] * jnp.where(mask, 1.0, 0.0).astype(jnp.bfloat16))
            w = jnp.concatenate(parts, axis=0)
            acc[rows, :] += jnp.dot(w, kv[rows, DH : 2 * DH], preferred_element_type=jnp.float32)

    if not last:
        out_ref[...] = acc[...]
    else:
        for s in range(NY):
            event = (s * NZ + z) * ROWS
            at = lax.broadcasted_iota(jnp.int32, (ROWS, DH), 0)
            stop = jnp.where(at < BLOCK, stops[2 * s], stops[2 * s + 1])
            rows = jnp.where(event + at < stop, acc[s * ROWS : (s + 1) * ROWS, :], 0.0).astype(jnp.bfloat16)
            out_ref[s * FOLD : (s + 1) * FOLD, 0:DH] = rows[0:FOLD]
            out_ref[s * FOLD : s * FOLD + REST, DH : 2 * DH] = rows[FOLD:ROWS]
            cands = acc[KEYS + s * CROWS : KEYS + (s + 1) * CROWS, :].astype(jnp.bfloat16)
            out_ref[s * FOLD + REST : (s + 1) * FOLD, DH : 2 * DH] = cands


def attend(offsets, info, queries, users, blocks, total, last=False):
    first = total is None
    shape = jax.ShapeDtypeStruct((NY * FOLD, 2 * DH), jnp.bfloat16) if last else jax.ShapeDtypeStruct((TOTAL, DH), jnp.float32)
    state = [] if first else [total]
    keys = len(offsets) * KEYS
    return pl.pallas_call(
        functools.partial(attend_kernel, offsets, first, last),
        in_specs=[SMEM] + [VMEM] * (2 + len(blocks) + len(state)),
        out_specs=VMEM,
        out_shape=shape,
        scratch_shapes=[pltpu.VMEM((keys, 2 * DH), jnp.bfloat16), pltpu.VMEM((TOTAL, DH), jnp.float32)],
        compiler_params=PARAMS,
        cost_estimate=pl.CostEstimate(flops=4 * TOTAL * keys * DH, bytes_accessed=1 << 20, transcendentals=0),
        name="attend",
    )(info, queries, users, *blocks, *state)


def finish_kernel(t_ref, hg, hx, cq, ck, cv, cg, cx, w_ref, ho, co):
    hist, cand = [], []
    for h in range(HEADS):
        at = slice(h * DH, (h + 1) * DH)
        rows = t_ref[h * FOLD : (h + 1) * FOLD, :].astype(jnp.float32)
        hist.append(jnp.concatenate([rows[:, 0:DH], rows[0:REST, DH : 2 * DH]], axis=0))
        scores = jnp.sum(cq[:, at].astype(jnp.float32) * ck[:, at].astype(jnp.float32), axis=-1, keepdims=True)
        weight = silu_weight(scores).astype(jnp.float32)
        cand.append(rows[REST:FOLD, DH : 2 * DH] + weight * cv[:, at].astype(jnp.float32))

    def tail(total, gate, inputs, out):
        mean = jnp.mean(total, axis=-1, keepdims=True)
        centered = total - mean
        spread = jnp.mean(centered * centered, axis=-1, keepdims=True)
        normed = centered * lax.rsqrt(spread + 1e-05)
        gated = (normed * gate[...].astype(jnp.float32)).astype(jnp.bfloat16)
        mixed = jnp.dot(gated, w_ref[...], preferred_element_type=jnp.float32)
        out[...] = (inputs[...].astype(jnp.float32) + mixed).astype(jnp.bfloat16)

    tail(jnp.concatenate(hist, axis=1), hg, hx, ho)
    tail(jnp.concatenate(cand, axis=1), cg, cx, co)


def call(kernel, shapes, *args, place=None, scratch=(), limit=VMEM_LIMIT):
    args = args if place is None else (place, *args)
    return pl.pallas_call(
        kernel,
        in_specs=[SMEM] * (place is not None) + [VMEM] * (len(args) - (place is not None)),
        out_specs=[VMEM] * len(shapes),
        out_shape=[jax.ShapeDtypeStruct(s, jnp.bfloat16) for s in shapes],
        scratch_shapes=scratch,
        compiler_params=pltpu.CompilerParams(vmem_limit_bytes=limit),
    )(*args)


def turn(array, axis, step):
    count = NY if axis == "y" else NZ
    return lax.ppermute(array, axis, [(i, (i + step) % count) for i in range(count)])


def on_device(
    hist_query, hist_key, hist_value, hist_gate, hist_input,
    cand_query, cand_key, cand_value, cand_gate, cand_input,
    cand_user, hist_len, hist_start, out_weight,
):
    z = lax.axis_index("z").astype(jnp.int32)
    y = lax.axis_index("y").astype(jnp.int32).reshape(1)
    info = jnp.concatenate([z.reshape(1), hist_start, hist_len])
    users = lax.dynamic_index_in_dim(cand_user.reshape(NY, NZ, CROWS), z, axis=1).reshape(NY * CROWS, 1)
    parts = call(
        split_kernel, [(ROWS, 2 * DH)] * HEADS + [(FOLD, 2 * DH)] * HEADS,
        hist_key, hist_value, hist_query, cand_query, place=y, limit=WIDE_LIMIT,
    )
    pieces = [parts[0]] + [turn(parts[i], "y", i) for i in (1, 2, 3)]
    (own,) = call(join_kernel, [(KEYS, 2 * DH)], *pieces, place=y)
    up1, down1 = turn(own, "z", 1), turn(own, "z", -1)
    folds = [parts[HEADS]] + [turn(parts[HEADS + i], "y", i) for i in (1, 2, 3)]
    up1, folds[1] = lax.optimization_barrier((up1, folds[1]))
    down1, folds[3] = lax.optimization_barrier((down1, folds[3]))
    up2, down2 = turn(up1, "z", 1), turn(down1, "z", -1)
    (queries,) = call(unfold_kernel, [(TOTAL, DH)], *folds, place=y)
    total = attend((0,), info, queries, users, (own,), None)
    total = attend((NZ - 1, 1), info, queries, users, (up1, down1), total)
    up2, held = lax.optimization_barrier((up2, total))
    down2, total = lax.optimization_barrier((down2, held))
    up3, down3 = turn(up2, "z", 1), turn(down2, "z", -1)
    total = attend((NZ - 2, 2), info, queries, users, (up2, down2), total)
    up3, total = lax.optimization_barrier((up3, total))
    across = turn(up3, "z", 1)
    total = attend((NZ - 3, 3), info, queries, users, (up3, down3), total)
    total = attend((4,), info, queries, users, (across,), total, last=True)
    total = lax.all_to_all(total, "y", 0, 0, tiled=True)
    return tuple(
        call(
            finish_kernel, [hist_input.shape, cand_input.shape],
            total, hist_gate, hist_input, cand_query, cand_key, cand_value, cand_gate, cand_input, out_weight,
        )
    )


def solution(mesh):
    grid = Mesh(mesh.devices.reshape(-1, NY, NZ), ("batch", "y", "z"))
    rows = P(("batch", "y", "z"), None)
    return jax.shard_map(
        on_device,
        mesh=grid,
        in_specs=(rows,) * 10 + (P("batch"), P("batch"), P("batch"), P()),
        out_specs=(rows, rows),
        check_vma=False,
    )
```

```python
import functools
import math

import jax
import jax.numpy as jnp
from jax import lax
from jax.experimental import pallas as pl
from jax.experimental.pallas import tpu as pltpu
from jax.sharding import Mesh, PartitionSpec as P

HEADS = 4
DH = 128
NY = 4
NZ = 8
ROWS = 256
CROWS = 32
QROWS = ROWS + CROWS
FOLD = QROWS // 2
REST = ROWS - FOLD
BLOCK = 128
KEYS = NY * ROWS
TOTAL = KEYS + NY * CROWS
NOBODY = 1 << 30
HALF = 1.0 / (2.0 * math.sqrt(DH))
VMEM_LIMIT = 16 * 1024 * 1024
WIDE_LIMIT = 60 * 1024 * 1024
VMEM = pl.BlockSpec(memory_space=pltpu.VMEM)
SMEM = pl.BlockSpec(memory_space=pltpu.SMEM)
PARAMS = pltpu.CompilerParams(vmem_limit_bytes=VMEM_LIMIT)


def contract_lanes(a, b):
    return lax.dot_general(a, b, (((1,), (1,)), ((), ())), preferred_element_type=jnp.float32)


def silu_weight(scores):
    half = scores * HALF
    return (half * jnp.tanh(half) + half).astype(jnp.bfloat16)


def split_kernel(y_ref, k_ref, v_ref, q_ref, c_ref, *outs):
    for i in range(HEADS):
        at = pl.ds(pl.multiple_of(lax.rem(y_ref[0] + i, HEADS) * DH, DH), DH)
        kv, q = outs[i], outs[HEADS + i]
        kv[:, 0:DH] = k_ref[:, at]
        kv[:, DH : 2 * DH] = v_ref[:, at]
        q[:, 0:DH] = q_ref[0:FOLD, at]
        q[0:REST, DH : 2 * DH] = q_ref[FOLD:ROWS, at]
        q[REST:FOLD, DH : 2 * DH] = c_ref[:, at]


def join_kernel(y_ref, *refs):
    *pieces, out = refs
    for i, piece in enumerate(pieces):
        strip = lax.rem(y_ref[0] + NY - i, NY)
        out[pl.ds(pl.multiple_of(strip * ROWS, ROWS), ROWS), :] = piece[...]


def unfold_kernel(y_ref, *refs):
    *pieces, out = refs
    for i, piece in enumerate(pieces):
        strip = lax.rem(y_ref[0] + NY - i, NY)
        row = pl.multiple_of(strip * ROWS, ROWS)
        out[pl.ds(row, FOLD), :] = piece[:, 0:DH]
        out[pl.ds(pl.multiple_of(row + FOLD, 16), REST), :] = piece[0:REST, DH : 2 * DH]
        out[pl.ds(pl.multiple_of(KEYS + strip * CROWS, CROWS), CROWS), :] = piece[REST:FOLD, DH : 2 * DH]


def attend_kernel(offsets, first, last, info_ref, qs, user_ref, *refs):
    *ins, out_ref, kv, acc = refs
    z = info_ref[0]
    starts = [info_ref[1 + u] for u in range(2)]
    ends = [info_ref[1 + u] + info_ref[3 + u] for u in range(2)]

    for i in range(len(offsets)):
        kv[i * KEYS : (i + 1) * KEYS, :] = ins[i][...]
    if first:
        acc[...] = jnp.zeros_like(acc)
    else:
        acc[...] = ins[-1][...]

    lows, stops = [], []
    for half in range(2 * NY):
        event = (half // 2 * NZ + z) * ROWS + half % 2 * BLOCK
        low, stop = jnp.int32(NOBODY), jnp.int32(0)
        for s, t in zip(starts, ends):
            inside = (s <= event) & (event < t)
            low = jnp.where(inside, s, low)
            stop = jnp.where(inside, t, stop)
        lows.append(low)
        stops.append(stop)
    user = user_ref[...]
    cand_low = jnp.where(user == 0, starts[0], starts[1])
    cand_stop = jnp.where(user == 0, ends[0], ends[1])
    column = lax.broadcasted_iota(jnp.int32, (1, ROWS), 1)

    def block_step(block, base, shift):
        for strip in range(NY):
            row = (strip + shift) * ROWS
            key = pl.multiple_of(base + strip * ROWS, ROWS)
            events = (strip * NZ + block) * ROWS + column
            w = silu_weight(contract_lanes(qs[row:TOTAL, :], kv[pl.ds(key, ROWS), 0:DH]))
            parts = []
            for half in range(2 * (strip + shift), 2 * NY):
                at = half * BLOCK - row
                keep = jnp.where(events >= lows[half], 1.0, 0.0).astype(jnp.bfloat16)
                parts.append(w[at : at + BLOCK] * keep)
            keep = jnp.where((events >= cand_low) & (events < cand_stop), 1.0, 0.0).astype(jnp.bfloat16)
            parts.append(w[KEYS - row :] * keep)
            w = parts[0] if len(parts) == 1 else jnp.concatenate(parts, axis=0)
            acc[row:TOTAL, :] += jnp.dot(w, kv[pl.ds(key, ROWS), DH : 2 * DH], preferred_element_type=jnp.float32)

    def step(part, carry):
        block = z + offsets[-1]
        for n, offset in enumerate(offsets[:-1]):
            block = jnp.where(part == n, z + offset, block)
        block = lax.rem(block, NZ)

        @pl.when(block < z)
        def _():
            block_step(block, part * KEYS, 0)

        @pl.when(block >= z)
        def _():
            block_step(block, part * KEYS, 1)

        return carry

    lax.fori_loop(0, len(offsets), step, 0)

    if first:
        at = lax.broadcasted_iota(jnp.int32, (BLOCK, ROWS), 0)
        to = lax.broadcasted_iota(jnp.int32, (BLOCK, ROWS), 1)
        for s in range(NY):
            rows = slice(s * ROWS, (s + 1) * ROWS)
            w = silu_weight(contract_lanes(qs[rows, :], kv[rows, 0:DH]))
            event = (s * NZ + z) * ROWS
            parts = []
            for half in range(2):
                mask = (to <= at + half * BLOCK) & (event + to >= lows[2 * s + half])
                parts.append(w[half * BLOCK : (half + 1) * BLOCK] * jnp.where(mask, 1.0, 0.0).astype(jnp.bfloat16))
            w = jnp.concatenate(parts, axis=0)
            acc[rows, :] += jnp.dot(w, kv[rows, DH : 2 * DH], preferred_element_type=jnp.float32)

    if not last:
        out_ref[...] = acc[...]
    else:
        for s in range(NY):
            event = (s * NZ + z) * ROWS
            at = lax.broadcasted_iota(jnp.int32, (ROWS, DH), 0)
            stop = jnp.where(at < BLOCK, stops[2 * s], stops[2 * s + 1])
            rows = jnp.where(event + at < stop, acc[s * ROWS : (s + 1) * ROWS, :], 0.0).astype(jnp.bfloat16)
            out_ref[s * FOLD : (s + 1) * FOLD, 0:DH] = rows[0:FOLD]
            out_ref[s * FOLD : s * FOLD + REST, DH : 2 * DH] = rows[FOLD:ROWS]
            cands = acc[KEYS + s * CROWS : KEYS + (s + 1) * CROWS, :].astype(jnp.bfloat16)
            out_ref[s * FOLD + REST : (s + 1) * FOLD, DH : 2 * DH] = cands


def attend(offsets, info, queries, users, blocks, total, last=False):
    first = total is None
    shape = jax.ShapeDtypeStruct((NY * FOLD, 2 * DH), jnp.bfloat16) if last else jax.ShapeDtypeStruct((TOTAL, DH), jnp.float32)
    state = [] if first else [total]
    keys = len(offsets) * KEYS
    return pl.pallas_call(
        functools.partial(attend_kernel, offsets, first, last),
        in_specs=[SMEM] + [VMEM] * (2 + len(blocks) + len(state)),
        out_specs=VMEM,
        out_shape=shape,
        scratch_shapes=[pltpu.VMEM((keys, 2 * DH), jnp.bfloat16), pltpu.VMEM((TOTAL, DH), jnp.float32)],
        compiler_params=PARAMS,
        cost_estimate=pl.CostEstimate(flops=4 * TOTAL * keys * DH, bytes_accessed=1 << 20, transcendentals=0),
        name="attend",
    )(info, queries, users, *blocks, *state)


def finish_kernel(t_ref, hg, hx, cq, ck, cv, cg, cx, w_ref, ho, co):
    hist, cand = [], []
    for h in range(HEADS):
        at = slice(h * DH, (h + 1) * DH)
        rows = t_ref[h * FOLD : (h + 1) * FOLD, :].astype(jnp.float32)
        hist.append(jnp.concatenate([rows[:, 0:DH], rows[0:REST, DH : 2 * DH]], axis=0))
        scores = jnp.sum(cq[:, at].astype(jnp.float32) * ck[:, at].astype(jnp.float32), axis=-1, keepdims=True)
        weight = silu_weight(scores).astype(jnp.float32)
        cand.append(rows[REST:FOLD, DH : 2 * DH] + weight * cv[:, at].astype(jnp.float32))

    def tail(total, gate, inputs, out):
        mean = jnp.mean(total, axis=-1, keepdims=True)
        centered = total - mean
        spread = jnp.mean(centered * centered, axis=-1, keepdims=True)
        normed = centered * lax.rsqrt(spread + 1e-05)
        gated = (normed * gate[...].astype(jnp.float32)).astype(jnp.bfloat16)
        mixed = jnp.dot(gated, w_ref[...], preferred_element_type=jnp.float32)
        out[...] = (inputs[...].astype(jnp.float32) + mixed).astype(jnp.bfloat16)

    tail(jnp.concatenate(hist, axis=1), hg, hx, ho)
    tail(jnp.concatenate(cand, axis=1), cg, cx, co)


def call(kernel, shapes, *args, place=None, scratch=(), limit=VMEM_LIMIT):
    args = args if place is None else (place, *args)
    return pl.pallas_call(
        kernel,
        in_specs=[SMEM] * (place is not None) + [VMEM] * (len(args) - (place is not None)),
        out_specs=[VMEM] * len(shapes),
        out_shape=[jax.ShapeDtypeStruct(s, jnp.bfloat16) for s in shapes],
        scratch_shapes=scratch,
        compiler_params=pltpu.CompilerParams(vmem_limit_bytes=limit),
    )(*args)


def turn(array, axis, step):
    count = NY if axis == "y" else NZ
    return lax.ppermute(array, axis, [(i, (i + step) % count) for i in range(count)])


def on_device(
    hist_query, hist_key, hist_value, hist_gate, hist_input,
    cand_query, cand_key, cand_value, cand_gate, cand_input,
    cand_user, hist_len, hist_start, out_weight,
):
    z = lax.axis_index("z").astype(jnp.int32)
    y = lax.axis_index("y").astype(jnp.int32).reshape(1)
    info = jnp.concatenate([z.reshape(1), hist_start, hist_len])
    users = lax.dynamic_index_in_dim(cand_user.reshape(NY, NZ, CROWS), z, axis=1).reshape(NY * CROWS, 1)
    parts = call(
        split_kernel, [(ROWS, 2 * DH)] * HEADS + [(FOLD, 2 * DH)] * HEADS,
        hist_key, hist_value, hist_query, cand_query, place=y, limit=WIDE_LIMIT,
    )
    pieces = [parts[0]] + [turn(parts[i], "y", i) for i in (1, 2, 3)]
    (own,) = call(join_kernel, [(KEYS, 2 * DH)], *pieces, place=y)
    up1, down1 = turn(own, "z", 1), turn(own, "z", -1)
    folds = [parts[HEADS]] + [turn(parts[HEADS + i], "y", i) for i in (1, 2, 3)]
    up1, folds[1] = lax.optimization_barrier((up1, folds[1]))
    down1, folds[3] = lax.optimization_barrier((down1, folds[3]))
    up2, down2 = turn(up1, "z", 1), turn(down1, "z", -1)
    (queries,) = call(unfold_kernel, [(TOTAL, DH)], *folds, place=y)
    total = attend((0,), info, queries, users, (own,), None)
    total = attend((NZ - 1, 1), info, queries, users, (up1, down1), total)
    up3, down3 = turn(up2, "z", 1), turn(down2, "z", -1)
    up3, total = lax.optimization_barrier((up3, total))
    across = turn(up3, "z", 1)
    total = attend((NZ - 2, 2), info, queries, users, (up2, down2), total)
    total = attend((NZ - 3, 3), info, queries, users, (up3, down3), total)
    total = attend((4,), info, queries, users, (across,), total, last=True)
    total = lax.all_to_all(total, "y", 0, 0, tiled=True)
    return tuple(
        call(
            finish_kernel, [hist_input.shape, cand_input.shape],
            total, hist_gate, hist_input, cand_query, cand_key, cand_value, cand_gate, cand_input, out_weight,
        )
    )


def solution(mesh):
    grid = Mesh(mesh.devices.reshape(-1, NY, NZ), ("batch", "y", "z"))
    rows = P(("batch", "y", "z"), None)
    return jax.shard_map(
        on_device,
        mesh=grid,
        in_specs=(rows,) * 10 + (P("batch"), P("batch"), P("batch"), P()),
        out_specs=(rows, rows),
        check_vma=False,
    )
```

```python
import functools
import math

import jax
import jax.numpy as jnp
from jax import lax
from jax.experimental import pallas as pl
from jax.experimental.pallas import tpu as pltpu
from jax.sharding import Mesh, PartitionSpec as P

HEADS = 4
DH = 128
NY = 4
NZ = 8
ROWS = 256
CROWS = 32
QROWS = ROWS + CROWS
FOLD = QROWS // 2
REST = ROWS - FOLD
BLOCK = 128
KEYS = NY * ROWS
TOTAL = KEYS + NY * CROWS
NOBODY = 1 << 30
HALF = 1.0 / (2.0 * math.sqrt(DH))
VMEM_LIMIT = 16 * 1024 * 1024
WIDE_LIMIT = 60 * 1024 * 1024
VMEM = pl.BlockSpec(memory_space=pltpu.VMEM)
SMEM = pl.BlockSpec(memory_space=pltpu.SMEM)
PARAMS = pltpu.CompilerParams(vmem_limit_bytes=VMEM_LIMIT)


def contract_lanes(a, b):
    return lax.dot_general(a, b, (((1,), (1,)), ((), ())), preferred_element_type=jnp.float32)


def silu_weight(scores):
    half = scores * HALF
    return (half * jnp.tanh(half) + half).astype(jnp.bfloat16)


def split_kernel(y_ref, k_ref, v_ref, q_ref, c_ref, *outs):
    for i in range(HEADS):
        at = pl.ds(pl.multiple_of(lax.rem(y_ref[0] + i, HEADS) * DH, DH), DH)
        kv, q = outs[i], outs[HEADS + i]
        kv[:, 0:DH] = k_ref[:, at]
        kv[:, DH : 2 * DH] = v_ref[:, at]
        q[:, 0:DH] = q_ref[0:FOLD, at]
        q[0:REST, DH : 2 * DH] = q_ref[FOLD:ROWS, at]
        q[REST:FOLD, DH : 2 * DH] = c_ref[:, at]


def join_kernel(y_ref, *refs):
    *pieces, out = refs
    for i, piece in enumerate(pieces):
        strip = lax.rem(y_ref[0] + NY - i, NY)
        out[pl.ds(pl.multiple_of(strip * ROWS, ROWS), ROWS), :] = piece[...]


def unfold_kernel(y_ref, *refs):
    *pieces, out = refs
    for i, piece in enumerate(pieces):
        strip = lax.rem(y_ref[0] + NY - i, NY)
        row = pl.multiple_of(strip * ROWS, ROWS)
        out[pl.ds(row, FOLD), :] = piece[:, 0:DH]
        out[pl.ds(pl.multiple_of(row + FOLD, 16), REST), :] = piece[0:REST, DH : 2 * DH]
        out[pl.ds(pl.multiple_of(KEYS + strip * CROWS, CROWS), CROWS), :] = piece[REST:FOLD, DH : 2 * DH]


def attend_kernel(offsets, first, last, info_ref, qs, user_ref, *refs):
    *ins, out_ref, kv, acc = refs
    z = info_ref[0]
    starts = [info_ref[1 + u] for u in range(2)]
    ends = [info_ref[1 + u] + info_ref[3 + u] for u in range(2)]

    for i in range(len(offsets)):
        kv[i * KEYS : (i + 1) * KEYS, :] = ins[i][...]
    if first:
        acc[...] = jnp.zeros_like(acc)
    else:
        acc[...] = ins[-1][...]

    lows, stops = [], []
    for half in range(2 * NY):
        event = (half // 2 * NZ + z) * ROWS + half % 2 * BLOCK
        low, stop = jnp.int32(NOBODY), jnp.int32(0)
        for s, t in zip(starts, ends):
            inside = (s <= event) & (event < t)
            low = jnp.where(inside, s, low)
            stop = jnp.where(inside, t, stop)
        lows.append(low)
        stops.append(stop)
    user = user_ref[...]
    cand_low = jnp.where(user == 0, starts[0], starts[1])
    cand_stop = jnp.where(user == 0, ends[0], ends[1])
    column = lax.broadcasted_iota(jnp.int32, (1, ROWS), 1)

    def block_step(block, base, shift):
        for strip in range(NY):
            row = (strip + shift) * ROWS
            key = pl.multiple_of(base + strip * ROWS, ROWS)
            events = (strip * NZ + block) * ROWS + column
            w = silu_weight(contract_lanes(qs[row:TOTAL, :], kv[pl.ds(key, ROWS), 0:DH]))
            parts = []
            for half in range(2 * (strip + shift), 2 * NY):
                at = half * BLOCK - row
                keep = jnp.where(events >= lows[half], 1.0, 0.0).astype(jnp.bfloat16)
                parts.append(w[at : at + BLOCK] * keep)
            keep = jnp.where((events >= cand_low) & (events < cand_stop), 1.0, 0.0).astype(jnp.bfloat16)
            parts.append(w[KEYS - row :] * keep)
            w = parts[0] if len(parts) == 1 else jnp.concatenate(parts, axis=0)
            acc[row:TOTAL, :] += jnp.dot(w, kv[pl.ds(key, ROWS), DH : 2 * DH], preferred_element_type=jnp.float32)

    def step(part, carry):
        block = z + offsets[-1]
        for n, offset in enumerate(offsets[:-1]):
            block = jnp.where(part == n, z + offset, block)
        block = lax.rem(block, NZ)

        @pl.when(block < z)
        def _():
            block_step(block, part * KEYS, 0)

        @pl.when(block >= z)
        def _():
            block_step(block, part * KEYS, 1)

        return carry

    lax.fori_loop(0, len(offsets), step, 0)

    if first:
        at = lax.broadcasted_iota(jnp.int32, (BLOCK, ROWS), 0)
        to = lax.broadcasted_iota(jnp.int32, (BLOCK, ROWS), 1)
        for s in range(NY):
            rows = slice(s * ROWS, (s + 1) * ROWS)
            w = silu_weight(contract_lanes(qs[rows, :], kv[rows, 0:DH]))
            event = (s * NZ + z) * ROWS
            parts = []
            for half in range(2):
                mask = (to <= at + half * BLOCK) & (event + to >= lows[2 * s + half])
                parts.append(w[half * BLOCK : (half + 1) * BLOCK] * jnp.where(mask, 1.0, 0.0).astype(jnp.bfloat16))
            w = jnp.concatenate(parts, axis=0)
            acc[rows, :] += jnp.dot(w, kv[rows, DH : 2 * DH], preferred_element_type=jnp.float32)

    if not last:
        out_ref[...] = acc[...]
    else:
        for s in range(NY):
            event = (s * NZ + z) * ROWS
            at = lax.broadcasted_iota(jnp.int32, (ROWS, DH), 0)
            stop = jnp.where(at < BLOCK, stops[2 * s], stops[2 * s + 1])
            rows = jnp.where(event + at < stop, acc[s * ROWS : (s + 1) * ROWS, :], 0.0).astype(jnp.bfloat16)
            out_ref[s * FOLD : (s + 1) * FOLD, 0:DH] = rows[0:FOLD]
            out_ref[s * FOLD : s * FOLD + REST, DH : 2 * DH] = rows[FOLD:ROWS]
            cands = acc[KEYS + s * CROWS : KEYS + (s + 1) * CROWS, :].astype(jnp.bfloat16)
            out_ref[s * FOLD + REST : (s + 1) * FOLD, DH : 2 * DH] = cands


def attend(offsets, info, queries, users, blocks, total, last=False):
    first = total is None
    shape = jax.ShapeDtypeStruct((NY * FOLD, 2 * DH), jnp.bfloat16) if last else jax.ShapeDtypeStruct((TOTAL, DH), jnp.float32)
    state = [] if first else [total]
    keys = len(offsets) * KEYS
    return pl.pallas_call(
        functools.partial(attend_kernel, offsets, first, last),
        in_specs=[SMEM] + [VMEM] * (2 + len(blocks) + len(state)),
        out_specs=VMEM,
        out_shape=shape,
        scratch_shapes=[pltpu.VMEM((keys, 2 * DH), jnp.bfloat16), pltpu.VMEM((TOTAL, DH), jnp.float32)],
        compiler_params=PARAMS,
        cost_estimate=pl.CostEstimate(flops=4 * TOTAL * keys * DH, bytes_accessed=1 << 20, transcendentals=0),
        name="attend",
    )(info, queries, users, *blocks, *state)


def finish_kernel(t_ref, hg, hx, cq, ck, cv, cg, cx, w_ref, ho, co):
    hist, cand = [], []
    for h in range(HEADS):
        at = slice(h * DH, (h + 1) * DH)
        rows = t_ref[h * FOLD : (h + 1) * FOLD, :].astype(jnp.float32)
        hist.append(jnp.concatenate([rows[:, 0:DH], rows[0:REST, DH : 2 * DH]], axis=0))
        scores = jnp.sum(cq[:, at].astype(jnp.float32) * ck[:, at].astype(jnp.float32), axis=-1, keepdims=True)
        weight = silu_weight(scores).astype(jnp.float32)
        cand.append(rows[REST:FOLD, DH : 2 * DH] + weight * cv[:, at].astype(jnp.float32))

    def tail(total, gate, inputs, out):
        mean = jnp.mean(total, axis=-1, keepdims=True)
        centered = total - mean
        spread = jnp.mean(centered * centered, axis=-1, keepdims=True)
        normed = centered * lax.rsqrt(spread + 1e-05)
        gated = (normed * gate[...].astype(jnp.float32)).astype(jnp.bfloat16)
        mixed = jnp.dot(gated, w_ref[...], preferred_element_type=jnp.float32)
        out[...] = (inputs[...].astype(jnp.float32) + mixed).astype(jnp.bfloat16)

    tail(jnp.concatenate(hist, axis=1), hg, hx, ho)
    tail(jnp.concatenate(cand, axis=1), cg, cx, co)


def call(kernel, shapes, *args, place=None, scratch=(), limit=VMEM_LIMIT):
    args = args if place is None else (place, *args)
    return pl.pallas_call(
        kernel,
        in_specs=[SMEM] * (place is not None) + [VMEM] * (len(args) - (place is not None)),
        out_specs=[VMEM] * len(shapes),
        out_shape=[jax.ShapeDtypeStruct(s, jnp.bfloat16) for s in shapes],
        scratch_shapes=scratch,
        compiler_params=pltpu.CompilerParams(vmem_limit_bytes=limit),
    )(*args)


def turn(array, axis, step):
    count = NY if axis == "y" else NZ
    return lax.ppermute(array, axis, [(i, (i + step) % count) for i in range(count)])


def on_device(
    hist_query, hist_key, hist_value, hist_gate, hist_input,
    cand_query, cand_key, cand_value, cand_gate, cand_input,
    cand_user, hist_len, hist_start, out_weight,
):
    z = lax.axis_index("z").astype(jnp.int32)
    y = lax.axis_index("y").astype(jnp.int32).reshape(1)
    info = jnp.concatenate([z.reshape(1), hist_start, hist_len])
    users = lax.dynamic_index_in_dim(cand_user.reshape(NY, NZ, CROWS), z, axis=1).reshape(NY * CROWS, 1)
    parts = call(
        split_kernel, [(ROWS, 2 * DH)] * HEADS + [(FOLD, 2 * DH)] * HEADS,
        hist_key, hist_value, hist_query, cand_query, place=y, limit=WIDE_LIMIT,
    )
    pieces = [parts[0]] + [turn(parts[i], "y", i) for i in (1, 2, 3)]
    (own,) = call(join_kernel, [(KEYS, 2 * DH)], *pieces, place=y)
    up1, down1 = turn(own, "z", 1), turn(own, "z", -1)
    folds = [parts[HEADS]] + [turn(parts[HEADS + i], "y", i) for i in (1, 2, 3)]
    up1, folds[1] = lax.optimization_barrier((up1, folds[1]))
    down1, folds[2], folds[3] = lax.optimization_barrier((down1, folds[2], folds[3]))
    up2, down2 = turn(up1, "z", 1), turn(down1, "z", -1)
    (queries,) = call(unfold_kernel, [(TOTAL, DH)], *folds, place=y)
    total = attend((0,), info, queries, users, (own,), None)
    total = attend((NZ - 1, 1), info, queries, users, (up1, down1), total)
    down2, total = lax.optimization_barrier((down2, total))
    up3, down3 = turn(up2, "z", 1), turn(down2, "z", -1)
    across = turn(up3, "z", 1)
    total = attend((NZ - 2, 2), info, queries, users, (up2, down2), total)
    total = attend((NZ - 3, 3), info, queries, users, (up3, down3), total)
    total = attend((4,), info, queries, users, (across,), total, last=True)
    total = lax.all_to_all(total, "y", 0, 0, tiled=True)
    return tuple(
        call(
            finish_kernel, [hist_input.shape, cand_input.shape],
            total, hist_gate, hist_input, cand_query, cand_key, cand_value, cand_gate, cand_input, out_weight,
        )
    )


def solution(mesh):
    grid = Mesh(mesh.devices.reshape(-1, NY, NZ), ("batch", "y", "z"))
    rows = P(("batch", "y", "z"), None)
    return jax.shard_map(
        on_device,
        mesh=grid,
        in_specs=(rows,) * 10 + (P("batch"), P("batch"), P("batch"), P()),
        out_specs=(rows, rows),
        check_vma=False,
    )
```

```python
import functools
import math

import jax
import jax.numpy as jnp
from jax import lax
from jax.experimental import pallas as pl
from jax.experimental.pallas import tpu as pltpu
from jax.sharding import Mesh, PartitionSpec as P

HEADS = 4
DH = 128
NY = 4
NZ = 8
ROWS = 256
CROWS = 32
QROWS = ROWS + CROWS
FOLD = QROWS // 2
REST = ROWS - FOLD
BLOCK = 128
KEYS = NY * ROWS
TOTAL = KEYS + NY * CROWS
NOBODY = 1 << 30
HALF = 1.0 / (2.0 * math.sqrt(DH))
VMEM_LIMIT = 16 * 1024 * 1024
WIDE_LIMIT = 60 * 1024 * 1024
VMEM = pl.BlockSpec(memory_space=pltpu.VMEM)
SMEM = pl.BlockSpec(memory_space=pltpu.SMEM)
PARAMS = pltpu.CompilerParams(vmem_limit_bytes=VMEM_LIMIT)


def contract_lanes(a, b):
    return lax.dot_general(a, b, (((1,), (1,)), ((), ())), preferred_element_type=jnp.float32)


def silu_weight(scores):
    half = scores * HALF
    return (half * jnp.tanh(half) + half).astype(jnp.bfloat16)


def split_kernel(y_ref, k_ref, v_ref, q_ref, c_ref, *outs):
    for i in range(HEADS):
        at = pl.ds(pl.multiple_of(lax.rem(y_ref[0] + i, HEADS) * DH, DH), DH)
        kv, q = outs[i], outs[HEADS + i]
        kv[:, 0:DH] = k_ref[:, at]
        kv[:, DH : 2 * DH] = v_ref[:, at]
        q[:, 0:DH] = q_ref[0:FOLD, at]
        q[0:REST, DH : 2 * DH] = q_ref[FOLD:ROWS, at]
        q[REST:FOLD, DH : 2 * DH] = c_ref[:, at]


def join_kernel(y_ref, *refs):
    *pieces, out = refs
    for i, piece in enumerate(pieces):
        strip = lax.rem(y_ref[0] + NY - i, NY)
        out[pl.ds(pl.multiple_of(strip * ROWS, ROWS), ROWS), :] = piece[...]


def unfold_kernel(y_ref, *refs):
    *pieces, out = refs
    for i, piece in enumerate(pieces):
        strip = lax.rem(y_ref[0] + NY - i, NY)
        row = pl.multiple_of(strip * ROWS, ROWS)
        out[pl.ds(row, FOLD), :] = piece[:, 0:DH]
        out[pl.ds(pl.multiple_of(row + FOLD, 16), REST), :] = piece[0:REST, DH : 2 * DH]
        out[pl.ds(pl.multiple_of(KEYS + strip * CROWS, CROWS), CROWS), :] = piece[REST:FOLD, DH : 2 * DH]


def attend_kernel(offsets, first, last, info_ref, qs, user_ref, *refs):
    *ins, out_ref, kv, acc = refs
    z = info_ref[0]
    starts = [info_ref[1 + u] for u in range(2)]
    ends = [info_ref[1 + u] + info_ref[3 + u] for u in range(2)]

    for i in range(len(offsets)):
        kv[i * KEYS : (i + 1) * KEYS, :] = ins[i][...]
    if first:
        acc[...] = jnp.zeros_like(acc)
    else:
        acc[...] = ins[-1][...]

    lows, stops = [], []
    for half in range(2 * NY):
        event = (half // 2 * NZ + z) * ROWS + half % 2 * BLOCK
        low, stop = jnp.int32(NOBODY), jnp.int32(0)
        for s, t in zip(starts, ends):
            inside = (s <= event) & (event < t)
            low = jnp.where(inside, s, low)
            stop = jnp.where(inside, t, stop)
        lows.append(low)
        stops.append(stop)
    user = user_ref[...]
    cand_low = jnp.where(user == 0, starts[0], starts[1])
    cand_stop = jnp.where(user == 0, ends[0], ends[1])
    column = lax.broadcasted_iota(jnp.int32, (1, ROWS), 1)

    def block_step(block, base, shift):
        for strip in range(NY):
            row = (strip + shift) * ROWS
            key = pl.multiple_of(base + strip * ROWS, ROWS)
            events = (strip * NZ + block) * ROWS + column
            w = silu_weight(contract_lanes(qs[row:TOTAL, :], kv[pl.ds(key, ROWS), 0:DH]))
            parts = []
            for half in range(2 * (strip + shift), 2 * NY):
                at = half * BLOCK - row
                keep = jnp.where(events >= lows[half], 1.0, 0.0).astype(jnp.bfloat16)
                parts.append(w[at : at + BLOCK] * keep)
            keep = jnp.where((events >= cand_low) & (events < cand_stop), 1.0, 0.0).astype(jnp.bfloat16)
            parts.append(w[KEYS - row :] * keep)
            w = parts[0] if len(parts) == 1 else jnp.concatenate(parts, axis=0)
            acc[row:TOTAL, :] += jnp.dot(w, kv[pl.ds(key, ROWS), DH : 2 * DH], preferred_element_type=jnp.float32)

    def step(part, carry):
        block = z + offsets[-1]
        for n, offset in enumerate(offsets[:-1]):
            block = jnp.where(part == n, z + offset, block)
        block = lax.rem(block, NZ)

        @pl.when(block < z)
        def _():
            block_step(block, part * KEYS, 0)

        @pl.when(block >= z)
        def _():
            block_step(block, part * KEYS, 1)

        return carry

    lax.fori_loop(0, len(offsets), step, 0)

    if first:
        at = lax.broadcasted_iota(jnp.int32, (BLOCK, ROWS), 0)
        to = lax.broadcasted_iota(jnp.int32, (BLOCK, ROWS), 1)
        for s in range(NY):
            rows = slice(s * ROWS, (s + 1) * ROWS)
            w = silu_weight(contract_lanes(qs[rows, :], kv[rows, 0:DH]))
            event = (s * NZ + z) * ROWS
            parts = []
            for half in range(2):
                mask = (to <= at + half * BLOCK) & (event + to >= lows[2 * s + half])
                parts.append(w[half * BLOCK : (half + 1) * BLOCK] * jnp.where(mask, 1.0, 0.0).astype(jnp.bfloat16))
            w = jnp.concatenate(parts, axis=0)
            acc[rows, :] += jnp.dot(w, kv[rows, DH : 2 * DH], preferred_element_type=jnp.float32)

    if not last:
        out_ref[...] = acc[...]
    else:
        for s in range(NY):
            event = (s * NZ + z) * ROWS
            at = lax.broadcasted_iota(jnp.int32, (ROWS, DH), 0)
            stop = jnp.where(at < BLOCK, stops[2 * s], stops[2 * s + 1])
            rows = jnp.where(event + at < stop, acc[s * ROWS : (s + 1) * ROWS, :], 0.0).astype(jnp.bfloat16)
            out_ref[s * FOLD : (s + 1) * FOLD, 0:DH] = rows[0:FOLD]
            out_ref[s * FOLD : s * FOLD + REST, DH : 2 * DH] = rows[FOLD:ROWS]
            cands = acc[KEYS + s * CROWS : KEYS + (s + 1) * CROWS, :].astype(jnp.bfloat16)
            out_ref[s * FOLD + REST : (s + 1) * FOLD, DH : 2 * DH] = cands


def attend(offsets, info, queries, users, blocks, total, last=False):
    first = total is None
    shape = jax.ShapeDtypeStruct((NY * FOLD, 2 * DH), jnp.bfloat16) if last else jax.ShapeDtypeStruct((TOTAL, DH), jnp.float32)
    state = [] if first else [total]
    keys = len(offsets) * KEYS
    return pl.pallas_call(
        functools.partial(attend_kernel, offsets, first, last),
        in_specs=[SMEM] + [VMEM] * (2 + len(blocks) + len(state)),
        out_specs=VMEM,
        out_shape=shape,
        scratch_shapes=[pltpu.VMEM((keys, 2 * DH), jnp.bfloat16), pltpu.VMEM((TOTAL, DH), jnp.float32)],
        compiler_params=PARAMS,
        cost_estimate=pl.CostEstimate(flops=4 * TOTAL * keys * DH, bytes_accessed=1 << 20, transcendentals=0),
        name="attend",
    )(info, queries, users, *blocks, *state)


def finish_kernel(t_ref, hg, hx, cq, ck, cv, cg, cx, w_ref, ho, co):
    hist, cand = [], []
    for h in range(HEADS):
        at = slice(h * DH, (h + 1) * DH)
        rows = t_ref[h * FOLD : (h + 1) * FOLD, :].astype(jnp.float32)
        hist.append(jnp.concatenate([rows[:, 0:DH], rows[0:REST, DH : 2 * DH]], axis=0))
        scores = jnp.sum(cq[:, at].astype(jnp.float32) * ck[:, at].astype(jnp.float32), axis=-1, keepdims=True)
        weight = silu_weight(scores).astype(jnp.float32)
        cand.append(rows[REST:FOLD, DH : 2 * DH] + weight * cv[:, at].astype(jnp.float32))

    def tail(total, gate, inputs, out):
        mean = jnp.mean(total, axis=-1, keepdims=True)
        centered = total - mean
        spread = jnp.mean(centered * centered, axis=-1, keepdims=True)
        normed = centered * lax.rsqrt(spread + 1e-05)
        gated = (normed * gate[...].astype(jnp.float32)).astype(jnp.bfloat16)
        mixed = jnp.dot(gated, w_ref[...], preferred_element_type=jnp.float32)
        out[...] = (inputs[...].astype(jnp.float32) + mixed).astype(jnp.bfloat16)

    tail(jnp.concatenate(hist, axis=1), hg, hx, ho)
    tail(jnp.concatenate(cand, axis=1), cg, cx, co)


def call(kernel, shapes, *args, place=None, scratch=(), limit=VMEM_LIMIT):
    args = args if place is None else (place, *args)
    return pl.pallas_call(
        kernel,
        in_specs=[SMEM] * (place is not None) + [VMEM] * (len(args) - (place is not None)),
        out_specs=[VMEM] * len(shapes),
        out_shape=[jax.ShapeDtypeStruct(s, jnp.bfloat16) for s in shapes],
        scratch_shapes=scratch,
        compiler_params=pltpu.CompilerParams(vmem_limit_bytes=limit),
    )(*args)


def turn(array, axis, step):
    count = NY if axis == "y" else NZ
    return lax.ppermute(array, axis, [(i, (i + step) % count) for i in range(count)])


def on_device(
    hist_query, hist_key, hist_value, hist_gate, hist_input,
    cand_query, cand_key, cand_value, cand_gate, cand_input,
    cand_user, hist_len, hist_start, out_weight,
):
    z = lax.axis_index("z").astype(jnp.int32)
    y = lax.axis_index("y").astype(jnp.int32).reshape(1)
    info = jnp.concatenate([z.reshape(1), hist_start, hist_len])
    users = lax.dynamic_index_in_dim(cand_user.reshape(NY, NZ, CROWS), z, axis=1).reshape(NY * CROWS, 1)
    parts = call(
        split_kernel, [(ROWS, 2 * DH)] * HEADS + [(FOLD, 2 * DH)] * HEADS,
        hist_key, hist_value, hist_query, cand_query, place=y, limit=WIDE_LIMIT,
    )
    pieces = [parts[0]] + [turn(parts[i], "y", i) for i in (1, 2, 3)]
    (own,) = call(join_kernel, [(KEYS, 2 * DH)], *pieces, place=y)
    up1, down1 = turn(own, "z", 1), turn(own, "z", -1)
    folds = [parts[HEADS]] + [turn(parts[HEADS + i], "y", i) for i in (1, 2, 3)]
    up1, folds[3] = lax.optimization_barrier((up1, folds[3]))
    down1, folds[1], folds[2] = lax.optimization_barrier((down1, folds[1], folds[2]))
    up2, down2 = turn(up1, "z", 1), turn(down1, "z", -1)
    (queries,) = call(unfold_kernel, [(TOTAL, DH)], *folds, place=y)
    total = attend((0,), info, queries, users, (own,), None)
    total = attend((NZ - 1, 1), info, queries, users, (up1, down1), total)
    down2, total = lax.optimization_barrier((down2, total))
    up3, down3 = turn(up2, "z", 1), turn(down2, "z", -1)
    across = turn(up3, "z", 1)
    total = attend((NZ - 2, 2), info, queries, users, (up2, down2), total)
    total = attend((NZ - 3, 3), info, queries, users, (up3, down3), total)
    total = attend((4,), info, queries, users, (across,), total, last=True)
    total = lax.all_to_all(total, "y", 0, 0, tiled=True)
    return tuple(
        call(
            finish_kernel, [hist_input.shape, cand_input.shape],
            total, hist_gate, hist_input, cand_query, cand_key, cand_value, cand_gate, cand_input, out_weight,
        )
    )


def solution(mesh):
    grid = Mesh(mesh.devices.reshape(-1, NY, NZ), ("batch", "y", "z"))
    rows = P(("batch", "y", "z"), None)
    return jax.shard_map(
        on_device,
        mesh=grid,
        in_specs=(rows,) * 10 + (P("batch"), P("batch"), P("batch"), P()),
        out_specs=(rows, rows),
        check_vma=False,
    )
```

```python
import functools
import math

import jax
import jax.numpy as jnp
from jax import lax
from jax.experimental import pallas as pl
from jax.experimental.pallas import tpu as pltpu
from jax.sharding import Mesh, PartitionSpec as P

HEADS = 4
DH = 128
NY = 4
NZ = 8
ROWS = 256
CROWS = 32
QROWS = ROWS + CROWS
FOLD = QROWS // 2
REST = ROWS - FOLD
BLOCK = 128
KEYS = NY * ROWS
TOTAL = KEYS + NY * CROWS
NOBODY = 1 << 30
HALF = 1.0 / (2.0 * math.sqrt(DH))
VMEM_LIMIT = 16 * 1024 * 1024
WIDE_LIMIT = 60 * 1024 * 1024
VMEM = pl.BlockSpec(memory_space=pltpu.VMEM)
SMEM = pl.BlockSpec(memory_space=pltpu.SMEM)
PARAMS = pltpu.CompilerParams(vmem_limit_bytes=VMEM_LIMIT)


def contract_lanes(a, b):
    return lax.dot_general(a, b, (((1,), (1,)), ((), ())), preferred_element_type=jnp.float32)


def silu_weight(scores):
    half = scores * HALF
    return (half * jnp.tanh(half) + half).astype(jnp.bfloat16)


def split_kernel(y_ref, k_ref, v_ref, q_ref, c_ref, *outs):
    for i in range(HEADS):
        at = pl.ds(pl.multiple_of(lax.rem(y_ref[0] + i, HEADS) * DH, DH), DH)
        kv, q = outs[i], outs[HEADS + i]
        kv[:, 0:DH] = k_ref[:, at]
        kv[:, DH : 2 * DH] = v_ref[:, at]
        q[:, 0:DH] = q_ref[0:FOLD, at]
        q[0:REST, DH : 2 * DH] = q_ref[FOLD:ROWS, at]
        q[REST:FOLD, DH : 2 * DH] = c_ref[:, at]


def join_kernel(y_ref, *refs):
    *pieces, out = refs
    for i, piece in enumerate(pieces):
        strip = lax.rem(y_ref[0] + NY - i, NY)
        out[pl.ds(pl.multiple_of(strip * ROWS, ROWS), ROWS), :] = piece[...]


def unfold_kernel(y_ref, *refs):
    *pieces, out = refs
    for i, piece in enumerate(pieces):
        strip = lax.rem(y_ref[0] + NY - i, NY)
        row = pl.multiple_of(strip * ROWS, ROWS)
        out[pl.ds(row, FOLD), :] = piece[:, 0:DH]
        out[pl.ds(pl.multiple_of(row + FOLD, 16), REST), :] = piece[0:REST, DH : 2 * DH]
        out[pl.ds(pl.multiple_of(KEYS + strip * CROWS, CROWS), CROWS), :] = piece[REST:FOLD, DH : 2 * DH]


def attend_kernel(offsets, first, last, info_ref, qs, user_ref, *refs):
    *ins, out_ref, kv, acc = refs
    z = info_ref[0]
    starts = [info_ref[1 + u] for u in range(2)]
    ends = [info_ref[1 + u] + info_ref[3 + u] for u in range(2)]

    for i in range(len(offsets)):
        kv[i * KEYS : (i + 1) * KEYS, :] = ins[i][...]
    if first:
        acc[...] = jnp.zeros_like(acc)
    else:
        acc[...] = ins[-1][...]

    lows, stops = [], []
    for half in range(2 * NY):
        event = (half // 2 * NZ + z) * ROWS + half % 2 * BLOCK
        low, stop = jnp.int32(NOBODY), jnp.int32(0)
        for s, t in zip(starts, ends):
            inside = (s <= event) & (event < t)
            low = jnp.where(inside, s, low)
            stop = jnp.where(inside, t, stop)
        lows.append(low)
        stops.append(stop)
    user = user_ref[...]
    cand_low = jnp.where(user == 0, starts[0], starts[1])
    cand_stop = jnp.where(user == 0, ends[0], ends[1])
    column = lax.broadcasted_iota(jnp.int32, (1, ROWS), 1)

    def block_step(block, base, shift):
        for strip in range(NY):
            row = (strip + shift) * ROWS
            key = pl.multiple_of(base + strip * ROWS, ROWS)
            events = (strip * NZ + block) * ROWS + column
            w = silu_weight(contract_lanes(qs[row:TOTAL, :], kv[pl.ds(key, ROWS), 0:DH]))
            parts = []
            for half in range(2 * (strip + shift), 2 * NY):
                at = half * BLOCK - row
                keep = jnp.where(events >= lows[half], 1.0, 0.0).astype(jnp.bfloat16)
                parts.append(w[at : at + BLOCK] * keep)
            keep = jnp.where((events >= cand_low) & (events < cand_stop), 1.0, 0.0).astype(jnp.bfloat16)
            parts.append(w[KEYS - row :] * keep)
            w = parts[0] if len(parts) == 1 else jnp.concatenate(parts, axis=0)
            acc[row:TOTAL, :] += jnp.dot(w, kv[pl.ds(key, ROWS), DH : 2 * DH], preferred_element_type=jnp.float32)

    def step(part, carry):
        block = z + offsets[-1]
        for n, offset in enumerate(offsets[:-1]):
            block = jnp.where(part == n, z + offset, block)
        block = lax.rem(block, NZ)

        @pl.when(block < z)
        def _():
            block_step(block, part * KEYS, 0)

        @pl.when(block >= z)
        def _():
            block_step(block, part * KEYS, 1)

        return carry

    lax.fori_loop(0, len(offsets), step, 0)

    if first:
        at = lax.broadcasted_iota(jnp.int32, (BLOCK, ROWS), 0)
        to = lax.broadcasted_iota(jnp.int32, (BLOCK, ROWS), 1)
        for s in range(NY):
            rows = slice(s * ROWS, (s + 1) * ROWS)
            w = silu_weight(contract_lanes(qs[rows, :], kv[rows, 0:DH]))
            event = (s * NZ + z) * ROWS
            parts = []
            for half in range(2):
                mask = (to <= at + half * BLOCK) & (event + to >= lows[2 * s + half])
                parts.append(w[half * BLOCK : (half + 1) * BLOCK] * jnp.where(mask, 1.0, 0.0).astype(jnp.bfloat16))
            w = jnp.concatenate(parts, axis=0)
            acc[rows, :] += jnp.dot(w, kv[rows, DH : 2 * DH], preferred_element_type=jnp.float32)

    if not last:
        out_ref[...] = acc[...]
    else:
        for s in range(NY):
            event = (s * NZ + z) * ROWS
            at = lax.broadcasted_iota(jnp.int32, (ROWS, DH), 0)
            stop = jnp.where(at < BLOCK, stops[2 * s], stops[2 * s + 1])
            rows = jnp.where(event + at < stop, acc[s * ROWS : (s + 1) * ROWS, :], 0.0).astype(jnp.bfloat16)
            out_ref[s * FOLD : (s + 1) * FOLD, 0:DH] = rows[0:FOLD]
            out_ref[s * FOLD : s * FOLD + REST, DH : 2 * DH] = rows[FOLD:ROWS]
            cands = acc[KEYS + s * CROWS : KEYS + (s + 1) * CROWS, :].astype(jnp.bfloat16)
            out_ref[s * FOLD + REST : (s + 1) * FOLD, DH : 2 * DH] = cands


def attend(offsets, info, queries, users, blocks, total, last=False):
    first = total is None
    shape = jax.ShapeDtypeStruct((NY * FOLD, 2 * DH), jnp.bfloat16) if last else jax.ShapeDtypeStruct((TOTAL, DH), jnp.float32)
    state = [] if first else [total]
    keys = len(offsets) * KEYS
    return pl.pallas_call(
        functools.partial(attend_kernel, offsets, first, last),
        in_specs=[SMEM] + [VMEM] * (2 + len(blocks) + len(state)),
        out_specs=VMEM,
        out_shape=shape,
        scratch_shapes=[pltpu.VMEM((keys, 2 * DH), jnp.bfloat16), pltpu.VMEM((TOTAL, DH), jnp.float32)],
        compiler_params=PARAMS,
        cost_estimate=pl.CostEstimate(flops=4 * TOTAL * keys * DH, bytes_accessed=1 << 20, transcendentals=0),
        name="attend",
    )(info, queries, users, *blocks, *state)


def finish_kernel(t_ref, hg, hx, cq, ck, cv, cg, cx, w_ref, ho, co):
    hist, cand = [], []
    for h in range(HEADS):
        at = slice(h * DH, (h + 1) * DH)
        rows = t_ref[h * FOLD : (h + 1) * FOLD, :].astype(jnp.float32)
        hist.append(jnp.concatenate([rows[:, 0:DH], rows[0:REST, DH : 2 * DH]], axis=0))
        scores = jnp.sum(cq[:, at].astype(jnp.float32) * ck[:, at].astype(jnp.float32), axis=-1, keepdims=True)
        weight = silu_weight(scores).astype(jnp.float32)
        cand.append(rows[REST:FOLD, DH : 2 * DH] + weight * cv[:, at].astype(jnp.float32))

    def tail(total, gate, inputs, out):
        mean = jnp.mean(total, axis=-1, keepdims=True)
        centered = total - mean
        spread = jnp.mean(centered * centered, axis=-1, keepdims=True)
        normed = centered * lax.rsqrt(spread + 1e-05)
        gated = (normed * gate[...].astype(jnp.float32)).astype(jnp.bfloat16)
        mixed = jnp.dot(gated, w_ref[...], preferred_element_type=jnp.float32)
        out[...] = (inputs[...].astype(jnp.float32) + mixed).astype(jnp.bfloat16)

    tail(jnp.concatenate(hist, axis=1), hg, hx, ho)
    tail(jnp.concatenate(cand, axis=1), cg, cx, co)


def call(kernel, shapes, *args, place=None, scratch=(), limit=VMEM_LIMIT):
    args = args if place is None else (place, *args)
    return pl.pallas_call(
        kernel,
        in_specs=[SMEM] * (place is not None) + [VMEM] * (len(args) - (place is not None)),
        out_specs=[VMEM] * len(shapes),
        out_shape=[jax.ShapeDtypeStruct(s, jnp.bfloat16) for s in shapes],
        scratch_shapes=scratch,
        compiler_params=pltpu.CompilerParams(vmem_limit_bytes=limit),
    )(*args)


def turn(array, axis, step):
    count = NY if axis == "y" else NZ
    return lax.ppermute(array, axis, [(i, (i + step) % count) for i in range(count)])


def on_device(
    hist_query, hist_key, hist_value, hist_gate, hist_input,
    cand_query, cand_key, cand_value, cand_gate, cand_input,
    cand_user, hist_len, hist_start, out_weight,
):
    z = lax.axis_index("z").astype(jnp.int32)
    y = lax.axis_index("y").astype(jnp.int32).reshape(1)
    info = jnp.concatenate([z.reshape(1), hist_start, hist_len])
    users = lax.dynamic_index_in_dim(cand_user.reshape(NY, NZ, CROWS), z, axis=1).reshape(NY * CROWS, 1)
    parts = call(
        split_kernel, [(ROWS, 2 * DH)] * HEADS + [(FOLD, 2 * DH)] * HEADS,
        hist_key, hist_value, hist_query, cand_query, place=y, limit=WIDE_LIMIT,
    )
    pieces = [parts[0]] + [turn(parts[i], "y", i) for i in (1, 2, 3)]
    (own,) = call(join_kernel, [(KEYS, 2 * DH)], *pieces, place=y)
    up1, down1 = turn(own, "z", 1), turn(own, "z", -1)
    folds = [parts[HEADS]] + [turn(parts[HEADS + i], "y", i) for i in (1, 2, 3)]
    up1, folds[3] = lax.optimization_barrier((up1, folds[3]))
    down1, folds[1] = lax.optimization_barrier((down1, folds[1]))
    up2, down2 = turn(up1, "z", 1), turn(down1, "z", -1)
    (queries,) = call(unfold_kernel, [(TOTAL, DH)], *folds, place=y)
    total = attend((0,), info, queries, users, (own,), None)
    down2, total = lax.optimization_barrier((down2, total))
    up3, down3 = turn(up2, "z", 1), turn(down2, "z", -1)
    across = turn(up3, "z", 1)
    total = attend((NZ - 1, 1), info, queries, users, (up1, down1), total)
    total = attend((NZ - 2, 2), info, queries, users, (up2, down2), total)
    total = attend((NZ - 3, 3), info, queries, users, (up3, down3), total)
    total = attend((4,), info, queries, users, (across,), total, last=True)
    total = lax.all_to_all(total, "y", 0, 0, tiled=True)
    return tuple(
        call(
            finish_kernel, [hist_input.shape, cand_input.shape],
            total, hist_gate, hist_input, cand_query, cand_key, cand_value, cand_gate, cand_input, out_weight,
        )
    )


def solution(mesh):
    grid = Mesh(mesh.devices.reshape(-1, NY, NZ), ("batch", "y", "z"))
    rows = P(("batch", "y", "z"), None)
    return jax.shard_map(
        on_device,
        mesh=grid,
        in_specs=(rows,) * 10 + (P("batch"), P("batch"), P("batch"), P()),
        out_specs=(rows, rows),
        check_vma=False,
    )
```

```python
import functools
import math

import jax
import jax.numpy as jnp
from jax import lax
from jax.experimental import pallas as pl
from jax.experimental.pallas import tpu as pltpu
from jax.sharding import Mesh, PartitionSpec as P

HEADS = 4
DH = 128
NY = 4
NZ = 8
ROWS = 256
CROWS = 32
QROWS = ROWS + CROWS
FOLD = QROWS // 2
REST = ROWS - FOLD
BLOCK = 128
KEYS = NY * ROWS
TOTAL = KEYS + NY * CROWS
NOBODY = 1 << 30
HALF = 1.0 / (2.0 * math.sqrt(DH))
VMEM_LIMIT = 16 * 1024 * 1024
WIDE_LIMIT = 60 * 1024 * 1024
VMEM = pl.BlockSpec(memory_space=pltpu.VMEM)
SMEM = pl.BlockSpec(memory_space=pltpu.SMEM)
PARAMS = pltpu.CompilerParams(vmem_limit_bytes=VMEM_LIMIT)


def contract_lanes(a, b):
    return lax.dot_general(a, b, (((1,), (1,)), ((), ())), preferred_element_type=jnp.float32)


def silu_weight(scores):
    half = scores * HALF
    return (half * jnp.tanh(half) + half).astype(jnp.bfloat16)


def split_kernel(y_ref, k_ref, v_ref, q_ref, c_ref, *outs):
    for i in range(HEADS):
        at = pl.ds(pl.multiple_of(lax.rem(y_ref[0] + i, HEADS) * DH, DH), DH)
        kv, q = outs[i], outs[HEADS + i]
        kv[:, 0:DH] = k_ref[:, at]
        kv[:, DH : 2 * DH] = v_ref[:, at]
        q[:, 0:DH] = q_ref[0:FOLD, at]
        q[0:REST, DH : 2 * DH] = q_ref[FOLD:ROWS, at]
        q[REST:FOLD, DH : 2 * DH] = c_ref[:, at]


def join_kernel(y_ref, *refs):
    *pieces, out = refs
    for i, piece in enumerate(pieces):
        strip = lax.rem(y_ref[0] + NY - i, NY)
        out[pl.ds(pl.multiple_of(strip * ROWS, ROWS), ROWS), :] = piece[...]


def unfold_kernel(y_ref, *refs):
    *pieces, out = refs
    for i, piece in enumerate(pieces):
        strip = lax.rem(y_ref[0] + NY - i, NY)
        row = pl.multiple_of(strip * ROWS, ROWS)
        out[pl.ds(row, FOLD), :] = piece[:, 0:DH]
        out[pl.ds(pl.multiple_of(row + FOLD, 16), REST), :] = piece[0:REST, DH : 2 * DH]
        out[pl.ds(pl.multiple_of(KEYS + strip * CROWS, CROWS), CROWS), :] = piece[REST:FOLD, DH : 2 * DH]


def attend_kernel(offsets, first, last, info_ref, qs, user_ref, *refs):
    *ins, out_ref, kv, acc = refs
    z = info_ref[0]
    starts = [info_ref[1 + u] for u in range(2)]
    ends = [info_ref[1 + u] + info_ref[3 + u] for u in range(2)]

    for i in range(len(offsets)):
        kv[i * KEYS : (i + 1) * KEYS, :] = ins[i][...]
    if first:
        acc[...] = jnp.zeros_like(acc)
    else:
        acc[...] = ins[-1][...]

    lows, stops = [], []
    for half in range(2 * NY):
        event = (half // 2 * NZ + z) * ROWS + half % 2 * BLOCK
        low, stop = jnp.int32(NOBODY), jnp.int32(0)
        for s, t in zip(starts, ends):
            inside = (s <= event) & (event < t)
            low = jnp.where(inside, s, low)
            stop = jnp.where(inside, t, stop)
        lows.append(low)
        stops.append(stop)
    user = user_ref[...]
    cand_low = jnp.where(user == 0, starts[0], starts[1])
    cand_stop = jnp.where(user == 0, ends[0], ends[1])
    column = lax.broadcasted_iota(jnp.int32, (1, ROWS), 1)

    def block_step(block, base, shift):
        for strip in range(NY):
            row = (strip + shift) * ROWS
            key = pl.multiple_of(base + strip * ROWS, ROWS)
            events = (strip * NZ + block) * ROWS + column
            w = silu_weight(contract_lanes(qs[row:TOTAL, :], kv[pl.ds(key, ROWS), 0:DH]))
            parts = []
            for half in range(2 * (strip + shift), 2 * NY):
                at = half * BLOCK - row
                keep = jnp.where(events >= lows[half], 1.0, 0.0).astype(jnp.bfloat16)
                parts.append(w[at : at + BLOCK] * keep)
            keep = jnp.where((events >= cand_low) & (events < cand_stop), 1.0, 0.0).astype(jnp.bfloat16)
            parts.append(w[KEYS - row :] * keep)
            w = parts[0] if len(parts) == 1 else jnp.concatenate(parts, axis=0)
            acc[row:TOTAL, :] += jnp.dot(w, kv[pl.ds(key, ROWS), DH : 2 * DH], preferred_element_type=jnp.float32)

    def step(part, carry):
        block = z + offsets[-1]
        for n, offset in enumerate(offsets[:-1]):
            block = jnp.where(part == n, z + offset, block)
        block = lax.rem(block, NZ)

        @pl.when(block < z)
        def _():
            block_step(block, part * KEYS, 0)

        @pl.when(block >= z)
        def _():
            block_step(block, part * KEYS, 1)

        return carry

    lax.fori_loop(0, len(offsets), step, 0)

    if first:
        at = lax.broadcasted_iota(jnp.int32, (BLOCK, ROWS), 0)
        to = lax.broadcasted_iota(jnp.int32, (BLOCK, ROWS), 1)
        for s in range(NY):
            rows = slice(s * ROWS, (s + 1) * ROWS)
            w = silu_weight(contract_lanes(qs[rows, :], kv[rows, 0:DH]))
            event = (s * NZ + z) * ROWS
            parts = []
            for half in range(2):
                mask = (to <= at + half * BLOCK) & (event + to >= lows[2 * s + half])
                parts.append(w[half * BLOCK : (half + 1) * BLOCK] * jnp.where(mask, 1.0, 0.0).astype(jnp.bfloat16))
            w = jnp.concatenate(parts, axis=0)
            acc[rows, :] += jnp.dot(w, kv[rows, DH : 2 * DH], preferred_element_type=jnp.float32)

    if not last:
        out_ref[...] = acc[...]
    else:
        for s in range(NY):
            event = (s * NZ + z) * ROWS
            at = lax.broadcasted_iota(jnp.int32, (ROWS, DH), 0)
            stop = jnp.where(at < BLOCK, stops[2 * s], stops[2 * s + 1])
            rows = jnp.where(event + at < stop, acc[s * ROWS : (s + 1) * ROWS, :], 0.0).astype(jnp.bfloat16)
            out_ref[s * FOLD : (s + 1) * FOLD, 0:DH] = rows[0:FOLD]
            out_ref[s * FOLD : s * FOLD + REST, DH : 2 * DH] = rows[FOLD:ROWS]
            cands = acc[KEYS + s * CROWS : KEYS + (s + 1) * CROWS, :].astype(jnp.bfloat16)
            out_ref[s * FOLD + REST : (s + 1) * FOLD, DH : 2 * DH] = cands


def attend(offsets, info, queries, users, blocks, total, last=False):
    first = total is None
    shape = jax.ShapeDtypeStruct((NY * FOLD, 2 * DH), jnp.bfloat16) if last else jax.ShapeDtypeStruct((TOTAL, DH), jnp.float32)
    state = [] if first else [total]
    keys = len(offsets) * KEYS
    return pl.pallas_call(
        functools.partial(attend_kernel, offsets, first, last),
        in_specs=[SMEM] + [VMEM] * (2 + len(blocks) + len(state)),
        out_specs=VMEM,
        out_shape=shape,
        scratch_shapes=[pltpu.VMEM((keys, 2 * DH), jnp.bfloat16), pltpu.VMEM((TOTAL, DH), jnp.float32)],
        compiler_params=PARAMS,
        cost_estimate=pl.CostEstimate(flops=4 * TOTAL * keys * DH, bytes_accessed=1 << 20, transcendentals=0),
        name="attend",
    )(info, queries, users, *blocks, *state)


def finish_kernel(t_ref, hg, hx, cq, ck, cv, cg, cx, w_ref, ho, co):
    hist, cand = [], []
    for h in range(HEADS):
        at = slice(h * DH, (h + 1) * DH)
        rows = t_ref[h * FOLD : (h + 1) * FOLD, :].astype(jnp.float32)
        hist.append(jnp.concatenate([rows[:, 0:DH], rows[0:REST, DH : 2 * DH]], axis=0))
        scores = jnp.sum(cq[:, at].astype(jnp.float32) * ck[:, at].astype(jnp.float32), axis=-1, keepdims=True)
        weight = silu_weight(scores).astype(jnp.float32)
        cand.append(rows[REST:FOLD, DH : 2 * DH] + weight * cv[:, at].astype(jnp.float32))

    def tail(total, gate, inputs, out):
        mean = jnp.mean(total, axis=-1, keepdims=True)
        centered = total - mean
        spread = jnp.mean(centered * centered, axis=-1, keepdims=True)
        normed = centered * lax.rsqrt(spread + 1e-05)
        gated = (normed * gate[...].astype(jnp.float32)).astype(jnp.bfloat16)
        mixed = jnp.dot(gated, w_ref[...], preferred_element_type=jnp.float32)
        out[...] = (inputs[...].astype(jnp.float32) + mixed).astype(jnp.bfloat16)

    tail(jnp.concatenate(hist, axis=1), hg, hx, ho)
    tail(jnp.concatenate(cand, axis=1), cg, cx, co)


def call(kernel, shapes, *args, place=None, scratch=(), limit=VMEM_LIMIT):
    args = args if place is None else (place, *args)
    return pl.pallas_call(
        kernel,
        in_specs=[SMEM] * (place is not None) + [VMEM] * (len(args) - (place is not None)),
        out_specs=[VMEM] * len(shapes),
        out_shape=[jax.ShapeDtypeStruct(s, jnp.bfloat16) for s in shapes],
        scratch_shapes=scratch,
        compiler_params=pltpu.CompilerParams(vmem_limit_bytes=limit),
    )(*args)


def turn(array, axis, step):
    count = NY if axis == "y" else NZ
    return lax.ppermute(array, axis, [(i, (i + step) % count) for i in range(count)])


def on_device(
    hist_query, hist_key, hist_value, hist_gate, hist_input,
    cand_query, cand_key, cand_value, cand_gate, cand_input,
    cand_user, hist_len, hist_start, out_weight,
):
    z = lax.axis_index("z").astype(jnp.int32)
    y = lax.axis_index("y").astype(jnp.int32).reshape(1)
    info = jnp.concatenate([z.reshape(1), hist_start, hist_len])
    users = lax.dynamic_index_in_dim(cand_user.reshape(NY, NZ, CROWS), z, axis=1).reshape(NY * CROWS, 1)
    parts = call(
        split_kernel, [(ROWS, 2 * DH)] * HEADS + [(FOLD, 2 * DH)] * HEADS,
        hist_key, hist_value, hist_query, cand_query, place=y, limit=WIDE_LIMIT,
    )
    pieces = [parts[0]] + [turn(parts[i], "y", i) for i in (1, 2, 3)]
    (own,) = call(join_kernel, [(KEYS, 2 * DH)], *pieces, place=y)
    up1, down1 = turn(own, "z", 1), turn(own, "z", -1)
    folds = [parts[HEADS]] + [turn(parts[HEADS + i], "y", i) for i in (1, 2, 3)]
    up1, folds[3] = lax.optimization_barrier((up1, folds[3]))
    down1, folds[1] = lax.optimization_barrier((down1, folds[1]))
    up2, down2 = turn(up1, "z", 1), turn(down1, "z", -1)
    down2, folds[2] = lax.optimization_barrier((down2, folds[2]))
    (queries,) = call(unfold_kernel, [(TOTAL, DH)], *folds, place=y)
    up3, down3 = turn(up2, "z", 1), turn(down2, "z", -1)
    across = turn(up3, "z", 1)
    total = attend((0, NZ - 1, 1), info, queries, users, (own, up1, down1), None)
    total = attend((NZ - 2, 2), info, queries, users, (up2, down2), total)
    total = attend((NZ - 3, 3), info, queries, users, (up3, down3), total)
    total = attend((4,), info, queries, users, (across,), total, last=True)
    total = lax.all_to_all(total, "y", 0, 0, tiled=True)
    return tuple(
        call(
            finish_kernel, [hist_input.shape, cand_input.shape],
            total, hist_gate, hist_input, cand_query, cand_key, cand_value, cand_gate, cand_input, out_weight,
        )
    )


def solution(mesh):
    grid = Mesh(mesh.devices.reshape(-1, NY, NZ), ("batch", "y", "z"))
    rows = P(("batch", "y", "z"), None)
    return jax.shard_map(
        on_device,
        mesh=grid,
        in_specs=(rows,) * 10 + (P("batch"), P("batch"), P("batch"), P()),
        out_specs=(rows, rows),
        check_vma=False,
    )
```

```python
import functools
import math

import jax
import jax.numpy as jnp
from jax import lax
from jax.experimental import pallas as pl
from jax.experimental.pallas import tpu as pltpu
from jax.sharding import Mesh, PartitionSpec as P

HEADS = 4
DH = 128
NY = 4
NZ = 8
ROWS = 256
CROWS = 32
QROWS = ROWS + CROWS
FOLD = QROWS // 2
REST = ROWS - FOLD
BLOCK = 128
KEYS = NY * ROWS
TOTAL = KEYS + NY * CROWS
NOBODY = 1 << 30
HALF = 1.0 / (2.0 * math.sqrt(DH))
VMEM_LIMIT = 16 * 1024 * 1024
WIDE_LIMIT = 60 * 1024 * 1024
VMEM = pl.BlockSpec(memory_space=pltpu.VMEM)
SMEM = pl.BlockSpec(memory_space=pltpu.SMEM)
PARAMS = pltpu.CompilerParams(vmem_limit_bytes=VMEM_LIMIT)


def contract_lanes(a, b):
    return lax.dot_general(a, b, (((1,), (1,)), ((), ())), preferred_element_type=jnp.float32)


def silu_weight(scores):
    half = scores * HALF
    return (half * jnp.tanh(half) + half).astype(jnp.bfloat16)


def split_kernel(y_ref, k_ref, v_ref, q_ref, c_ref, *outs):
    for i in range(HEADS):
        at = pl.ds(pl.multiple_of(lax.rem(y_ref[0] + i, HEADS) * DH, DH), DH)
        kv, q = outs[i], outs[HEADS + i]
        kv[:, 0:DH] = k_ref[:, at]
        kv[:, DH : 2 * DH] = v_ref[:, at]
        q[:, 0:DH] = q_ref[0:FOLD, at]
        q[0:REST, DH : 2 * DH] = q_ref[FOLD:ROWS, at]
        q[REST:FOLD, DH : 2 * DH] = c_ref[:, at]


def join_kernel(y_ref, *refs):
    *pieces, out = refs
    for i, piece in enumerate(pieces):
        strip = lax.rem(y_ref[0] + NY - i, NY)
        out[pl.ds(pl.multiple_of(strip * ROWS, ROWS), ROWS), :] = piece[...]


def unfold_kernel(y_ref, *refs):
    *pieces, out = refs
    for i, piece in enumerate(pieces):
        strip = lax.rem(y_ref[0] + NY - i, NY)
        row = pl.multiple_of(strip * ROWS, ROWS)
        out[pl.ds(row, FOLD), :] = piece[:, 0:DH]
        out[pl.ds(pl.multiple_of(row + FOLD, 16), REST), :] = piece[0:REST, DH : 2 * DH]
        out[pl.ds(pl.multiple_of(KEYS + strip * CROWS, CROWS), CROWS), :] = piece[REST:FOLD, DH : 2 * DH]


def attend_kernel(offsets, first, last, info_ref, qs, user_ref, *refs):
    *ins, out_ref, kv, acc = refs
    z = info_ref[0]
    starts = [info_ref[1 + u] for u in range(2)]
    ends = [info_ref[1 + u] + info_ref[3 + u] for u in range(2)]

    for i in range(len(offsets)):
        kv[i * KEYS : (i + 1) * KEYS, :] = ins[i][...]
    if first:
        acc[...] = jnp.zeros_like(acc)
    else:
        acc[...] = ins[-1][...]

    lows, stops = [], []
    for half in range(2 * NY):
        event = (half // 2 * NZ + z) * ROWS + half % 2 * BLOCK
        low, stop = jnp.int32(NOBODY), jnp.int32(0)
        for s, t in zip(starts, ends):
            inside = (s <= event) & (event < t)
            low = jnp.where(inside, s, low)
            stop = jnp.where(inside, t, stop)
        lows.append(low)
        stops.append(stop)
    user = user_ref[...]
    cand_low = jnp.where(user == 0, starts[0], starts[1])
    cand_stop = jnp.where(user == 0, ends[0], ends[1])
    column = lax.broadcasted_iota(jnp.int32, (1, ROWS), 1)

    def block_step(block, base, shift):
        for strip in range(NY):
            row = (strip + shift) * ROWS
            key = pl.multiple_of(base + strip * ROWS, ROWS)
            events = (strip * NZ + block) * ROWS + column
            w = silu_weight(contract_lanes(qs[row:TOTAL, :], kv[pl.ds(key, ROWS), 0:DH]))
            parts = []
            for half in range(2 * (strip + shift), 2 * NY):
                at = half * BLOCK - row
                keep = jnp.where(events >= lows[half], 1.0, 0.0).astype(jnp.bfloat16)
                parts.append(w[at : at + BLOCK] * keep)
            keep = jnp.where((events >= cand_low) & (events < cand_stop), 1.0, 0.0).astype(jnp.bfloat16)
            parts.append(w[KEYS - row :] * keep)
            w = parts[0] if len(parts) == 1 else jnp.concatenate(parts, axis=0)
            acc[row:TOTAL, :] += jnp.dot(w, kv[pl.ds(key, ROWS), DH : 2 * DH], preferred_element_type=jnp.float32)

    def step(part, carry):
        block = z + offsets[-1]
        for n, offset in enumerate(offsets[:-1]):
            block = jnp.where(part == n, z + offset, block)
        block = lax.rem(block, NZ)

        @pl.when(block < z)
        def _():
            block_step(block, part * KEYS, 0)

        @pl.when(block >= z)
        def _():
            block_step(block, part * KEYS, 1)

        return carry

    lax.fori_loop(0, len(offsets), step, 0)

    if first:
        at = lax.broadcasted_iota(jnp.int32, (BLOCK, ROWS), 0)
        to = lax.broadcasted_iota(jnp.int32, (BLOCK, ROWS), 1)
        for s in range(NY):
            rows = slice(s * ROWS, (s + 1) * ROWS)
            w = silu_weight(contract_lanes(qs[rows, :], kv[rows, 0:DH]))
            event = (s * NZ + z) * ROWS
            parts = []
            for half in range(2):
                mask = (to <= at + half * BLOCK) & (event + to >= lows[2 * s + half])
                parts.append(w[half * BLOCK : (half + 1) * BLOCK] * jnp.where(mask, 1.0, 0.0).astype(jnp.bfloat16))
            w = jnp.concatenate(parts, axis=0)
            acc[rows, :] += jnp.dot(w, kv[rows, DH : 2 * DH], preferred_element_type=jnp.float32)

    if not last:
        out_ref[...] = acc[...]
    else:
        for s in range(NY):
            event = (s * NZ + z) * ROWS
            at = lax.broadcasted_iota(jnp.int32, (ROWS, DH), 0)
            stop = jnp.where(at < BLOCK, stops[2 * s], stops[2 * s + 1])
            rows = jnp.where(event + at < stop, acc[s * ROWS : (s + 1) * ROWS, :], 0.0).astype(jnp.bfloat16)
            out_ref[s * FOLD : (s + 1) * FOLD, 0:DH] = rows[0:FOLD]
            out_ref[s * FOLD : s * FOLD + REST, DH : 2 * DH] = rows[FOLD:ROWS]
            cands = acc[KEYS + s * CROWS : KEYS + (s + 1) * CROWS, :].astype(jnp.bfloat16)
            out_ref[s * FOLD + REST : (s + 1) * FOLD, DH : 2 * DH] = cands


def attend(offsets, info, queries, users, blocks, total, last=False):
    first = total is None
    shape = jax.ShapeDtypeStruct((NY * FOLD, 2 * DH), jnp.bfloat16) if last else jax.ShapeDtypeStruct((TOTAL, DH), jnp.float32)
    state = [] if first else [total]
    keys = len(offsets) * KEYS
    return pl.pallas_call(
        functools.partial(attend_kernel, offsets, first, last),
        in_specs=[SMEM] + [VMEM] * (2 + len(blocks) + len(state)),
        out_specs=VMEM,
        out_shape=shape,
        scratch_shapes=[pltpu.VMEM((keys, 2 * DH), jnp.bfloat16), pltpu.VMEM((TOTAL, DH), jnp.float32)],
        compiler_params=PARAMS,
        cost_estimate=pl.CostEstimate(flops=4 * TOTAL * keys * DH, bytes_accessed=1 << 20, transcendentals=0),
        name="attend",
    )(info, queries, users, *blocks, *state)


def finish_kernel(t_ref, hg, hx, cq, ck, cv, cg, cx, w_ref, ho, co):
    hist, cand = [], []
    for h in range(HEADS):
        at = slice(h * DH, (h + 1) * DH)
        rows = t_ref[h * FOLD : (h + 1) * FOLD, :].astype(jnp.float32)
        hist.append(jnp.concatenate([rows[:, 0:DH], rows[0:REST, DH : 2 * DH]], axis=0))
        scores = jnp.sum(cq[:, at].astype(jnp.float32) * ck[:, at].astype(jnp.float32), axis=-1, keepdims=True)
        weight = silu_weight(scores).astype(jnp.float32)
        cand.append(rows[REST:FOLD, DH : 2 * DH] + weight * cv[:, at].astype(jnp.float32))

    def tail(total, gate, inputs, out):
        mean = jnp.mean(total, axis=-1, keepdims=True)
        centered = total - mean
        spread = jnp.mean(centered * centered, axis=-1, keepdims=True)
        normed = centered * lax.rsqrt(spread + 1e-05)
        gated = (normed * gate[...].astype(jnp.float32)).astype(jnp.bfloat16)
        mixed = jnp.dot(gated, w_ref[...], preferred_element_type=jnp.float32)
        out[...] = (inputs[...].astype(jnp.float32) + mixed).astype(jnp.bfloat16)

    tail(jnp.concatenate(hist, axis=1), hg, hx, ho)
    tail(jnp.concatenate(cand, axis=1), cg, cx, co)


def call(kernel, shapes, *args, place=None, scratch=(), limit=VMEM_LIMIT):
    args = args if place is None else (place, *args)
    return pl.pallas_call(
        kernel,
        in_specs=[SMEM] * (place is not None) + [VMEM] * (len(args) - (place is not None)),
        out_specs=[VMEM] * len(shapes),
        out_shape=[jax.ShapeDtypeStruct(s, jnp.bfloat16) for s in shapes],
        scratch_shapes=scratch,
        compiler_params=pltpu.CompilerParams(vmem_limit_bytes=limit),
    )(*args)


def turn(array, axis, step):
    count = NY if axis == "y" else NZ
    return lax.ppermute(array, axis, [(i, (i + step) % count) for i in range(count)])


def on_device(
    hist_query, hist_key, hist_value, hist_gate, hist_input,
    cand_query, cand_key, cand_value, cand_gate, cand_input,
    cand_user, hist_len, hist_start, out_weight,
):
    z = lax.axis_index("z").astype(jnp.int32)
    y = lax.axis_index("y").astype(jnp.int32).reshape(1)
    info = jnp.concatenate([z.reshape(1), hist_start, hist_len])
    users = lax.dynamic_index_in_dim(cand_user.reshape(NY, NZ, CROWS), z, axis=1).reshape(NY * CROWS, 1)
    parts = call(
        split_kernel, [(ROWS, 2 * DH)] * HEADS + [(FOLD, 2 * DH)] * HEADS,
        hist_key, hist_value, hist_query, cand_query, place=y, limit=WIDE_LIMIT,
    )
    pieces = [parts[0]] + [turn(parts[i], "y", i) for i in (1, 2, 3)]
    (own,) = call(join_kernel, [(KEYS, 2 * DH)], *pieces, place=y)
    up1, down1 = turn(own, "z", 1), turn(own, "z", -1)
    folds = [parts[HEADS]] + [turn(parts[HEADS + i], "y", i) for i in (1, 2, 3)]
    up1, folds[3] = lax.optimization_barrier((up1, folds[3]))
    down1, folds[1] = lax.optimization_barrier((down1, folds[1]))
    up2, down2 = turn(up1, "z", 1), turn(down1, "z", -1)
    down2, folds[2] = lax.optimization_barrier((down2, folds[2]))
    (queries,) = call(unfold_kernel, [(TOTAL, DH)], *folds, place=y)
    up3, down3 = turn(up2, "z", 1), turn(down2, "z", -1)
    across = turn(up3, "z", 1)
    total = attend((0, NZ - 1, 1, NZ - 2, 2), info, queries, users, (own, up1, down1, up2, down2), None)
    total = attend((NZ - 3, 3), info, queries, users, (up3, down3), total)
    total = attend((4,), info, queries, users, (across,), total, last=True)
    total = lax.all_to_all(total, "y", 0, 0, tiled=True)
    return tuple(
        call(
            finish_kernel, [hist_input.shape, cand_input.shape],
            total, hist_gate, hist_input, cand_query, cand_key, cand_value, cand_gate, cand_input, out_weight,
        )
    )


def solution(mesh):
    grid = Mesh(mesh.devices.reshape(-1, NY, NZ), ("batch", "y", "z"))
    rows = P(("batch", "y", "z"), None)
    return jax.shard_map(
        on_device,
        mesh=grid,
        in_specs=(rows,) * 10 + (P("batch"), P("batch"), P("batch"), P()),
        out_specs=(rows, rows),
        check_vma=False,
    )
```
